128 devices in a mesh: pts: 32 (over y, z, core), tp: 4 (over x).
Axes of the slice: x: 4, y: 4, z: 4, core: 2. Of those that a mesh axis runs over, the one named last changes fastest.
Arguments:
- points: bfloat16 [16384, 512], P('pts'), may hold values from -6 to 6
- destination: int32 [16384, 1], P('pts'), may hold values from 0 to 31; in each aligned block of 512 rows (0 to 511, 512 to 1023, ...) at most 32 rows name the same one
- pattern: int32 [256, 4], P('pts'), may hold values from 0 to 7, as said below
- norm_gain: float32 [512], replicated, may hold values from 0.5 to 1.5
- qkv_weight: bfloat16 [3, 512, 512], P(None, None, 'tp')
- out_weight: bfloat16 [512, 512], P('tp'), may hold values from -0.25 to 0.25
- grad_out: bfloat16 [16384, 512], P('pts'), may hold values from -6 to 6
Outputs:
- out: bfloat16 [16384, 512], P('pts')
- grad_input: bfloat16 [16384, 512], P('pts')
- grad_qkv: float32 [3, 512, 512], P(None, None, 'tp')
- grad_proj: float32 [512, 512], P('tp')
- grad_gain: float32 [512], replicated
The draws below stay inside these ranges and needn't reach their ends.
Inputs may be any that keep to these rules, and one draw needn't show every extreme that they name: `destination`: among the 512 points of one device no owner is named more than 32 times, and some owner exactly that often. `pattern`: row b of an owner's 8 rows names block b first, then 4 - 1 other distinct blocks of the same window of 1024 slots.
All inputs are finite; a program needn't handle non-finite values.
Results may differ from the reference program's by a relative error of at most 0.035.
Values may be sent and summed in bfloat16 or wider, within the bound.
A program may use at most 64 MiB of HBM per device.

```python
import math
import jax
import jax.numpy as jnp
import numpy as np
from jax import lax

D = 512
HEADS = 8
BLK = 128
WIN = 1024
KB = 4
P_DEV = 512
POINTS = 16384
C_SEND = 32
SLOTS = 1024
NBLK = 8
N_PTS = 32
N_TP = 4


def draw_pattern(key, part):
    blocks_win = WIN // BLK
    row_count = N_PTS * NBLK
    others = blocks_win - 1
    scores = jax.random.randint(key, (row_count, others), 0, 1 << 20) * others + jnp.arange(others, dtype=jnp.int32)[None, :]
    order = jnp.argsort(scores, axis=1).astype(jnp.int32)[:, :KB - 1]
    local = jnp.arange(row_count, dtype=jnp.int32) % NBLK
    itself = local % blocks_win
    start = local - itself
    picked = order + (order >= itself[:, None]).astype(jnp.int32)
    return jnp.concatenate([itself[:, None], picked], 1) + start[:, None]


def draw_qkv_weight(key, part):
    base = jax.random.normal(key, (3, D, D), jnp.float32) * D ** (-0.5)
    return base.astype(jnp.bfloat16)


def levels(key, extent, cuts, least, largest):
    def one(position, parts):
        heights = jax.random.uniform(jax.random.fold_in(jax.random.fold_in(key, 6), position), (parts,), jnp.float32, least / len(cuts), largest / len(cuts))
        return jnp.repeat(jnp.exp(heights), extent[position] // parts).reshape((-1,) + (1,) * (len(extent) - position - 1))

    loudness = one(*cuts[0])
    for cut in cuts[1:]:
        loudness = loudness * one(*cut)
    return loudness


def assign_block(rng, own, number, rows, amount, top, most, lean):
    ranking = jax.random.permutation(rng, amount)
    heavy_load, common = portions_of(amount, rows * top, most, lean, True), portions_of(amount, rows * top, most, lean, False)
    places = jnp.arange(amount)

    def named(lengths, rotation):
        used = int((lengths > 0).sum())
        fixed = max(1, used // 4)
        passed = fixed + (places - fixed + rotation * (used - fixed)) % max(1, amount - fixed)
        return jnp.zeros((amount,), jnp.int32).at[ranking[jnp.where(places < fixed, places, passed)]].set(jnp.asarray(lengths, jnp.int32))

    lengths = jnp.where(number % 4 == 0, named(heavy_load, number // 4), named(common, number - number // 4 - 1))
    mixed = jax.random.permutation(jax.random.fold_in(own, 3), amount)
    source_of, receiver = mixed[0:amount // 2 * 2:2], mixed[1:amount // 2 * 2:2]
    slack = jnp.minimum(lengths[source_of] - 1, most - lengths[receiver]) // 2
    slack = jnp.where((source_of == ranking[0]) | (receiver == ranking[0]) | (lengths[receiver] == 0), 0, jnp.maximum(slack, 0))
    passed = jax.random.randint(jax.random.fold_in(own, 4), (amount // 2,), 0, 1 << 20) % (slack + 1)
    lengths = lengths.at[source_of].add(-passed).at[receiver].add(passed)
    labels = jnp.searchsorted(jnp.cumsum(lengths), jnp.arange(rows * top), side="right").astype(jnp.int32)
    table = labels.reshape(top, rows).T
    table = table[jax.random.permutation(jax.random.fold_in(own, 1), rows)]
    rotation = jax.random.randint(jax.random.fold_in(own, 2), (rows, 1), 0, top)
    return jnp.take_along_axis(table, (jnp.arange(top)[None, :] + rotation) % top, axis=1)


def portions_of(number_of, total, limit, slope, full):
    loads = [(1 << 20) // math.isqrt(grade ** slope) + 1 for grade in range(1, number_of + 1)]
    largest = limit if full else min(limit, max(-(-total // number_of), total * loads[0] // sum(loads)))
    least = 1 if total - largest >= number_of - 1 else 0
    counts, spare = [largest] + [least] * (number_of - 1), total - largest - least * (number_of - 1)
    while spare > 0:
        movable = [i for i in range(1, number_of) if counts[i] < largest] or [i for i in range(1, number_of) if counts[i] < limit]
        whole, left = sum([loads[i] for i in movable]), spare
        for i in movable:
            addition = min(limit - counts[i], max(1, left * loads[i] // whole), spare)
            counts[i] = counts[i] + addition
            spare = spare - addition
    return np.array(counts)


def scatter_about(stream_key, extent, scale, bound, shards=(), kind=jnp.bfloat16):
    loudness = levels(stream_key, extent, shards, -0.22, 0.18) if shards else 1.0
    array = jax.random.normal(stream_key, extent, jnp.float32) * scale * loudness
    return jnp.minimum(jnp.maximum(array, -bound), bound).astype(kind)


def setup_inputs(seed: int = 0) -> dict:
    key_of = jax.random.split(jax.random.key(seed), 8)
    points = scatter_about(key_of[0], (POINTS, D), 1.0, 6.0, ((0, 32),))
    destination_keys = jax.random.split(jax.random.fold_in(key_of[1], 1), POINTS // P_DEV)
    destination_turns = jax.random.permutation(jax.random.fold_in(key_of[1], 3), POINTS // P_DEV)
    destination = jax.vmap(lambda own, number: assign_block(jax.random.fold_in(key_of[1], 2), own, number, P_DEV, N_PTS, 1, C_SEND, 2))(destination_keys, destination_turns).reshape((POINTS, 1))
    pattern = draw_pattern(jax.random.fold_in(key_of[7], 71), 0)
    norm_gain = jnp.clip(1.0 + 0.1 * jax.random.normal(key_of[3], (D,), jnp.float32), 0.5, 1.5)
    qkv_weight = draw_qkv_weight(jax.random.fold_in(key_of[7], 71), 0)
    out_weight = scatter_about(key_of[5], (D, D), D ** -0.5, 0.25, ((0, 4),))
    grad_out = scatter_about(key_of[6], (POINTS, D), 1.0, 6.0, ((0, 32),))
    return dict(points=points, destination=destination, pattern=pattern, norm_gain=norm_gain, qkv_weight=qkv_weight, out_weight=out_weight, grad_out=grad_out)


def norm_forward(features, norm_gain):
    as_float = features.astype(jnp.float32)
    center = lax.optimization_barrier(jnp.mean(as_float, -1, keepdims=True))
    shifted = as_float - center
    variance = lax.optimization_barrier(jnp.mean(shifted * shifted, -1, keepdims=True))
    inv_std = lax.rsqrt(variance + 1e-05)
    x_hat = shifted * inv_std
    return ((x_hat * norm_gain).astype(jnp.bfloat16), x_hat, inv_std)

def norm_backward(grad_normed, x_hat, inv_std, norm_gain):
    grad_float = grad_normed.astype(jnp.float32)
    scaled = grad_float * norm_gain
    first = lax.optimization_barrier(jnp.mean(scaled, -1, keepdims=True))
    second = lax.optimization_barrier(jnp.mean(scaled * x_hat, -1, keepdims=True))
    grad_branch = (inv_std * (scaled - first - x_hat * second)).astype(jnp.bfloat16)
    return (grad_branch, lax.optimization_barrier(jnp.sum(grad_float * x_hat, 0)))

def window_probs(queries, key_rows, key_live, query_live, scale):
    scores = jnp.einsum('bqhd,bkhd->bhqk', queries.astype(jnp.float32), key_rows.astype(jnp.float32)) * scale
    query_mask = query_live[:, None, :, None]
    visible = key_live[:, None, None, :] & query_mask
    masked = jnp.where(visible, scores, -1e+30)
    top_score = lax.optimization_barrier(jnp.max(masked, -1, keepdims=True))
    raised = jnp.where(visible, jnp.exp(masked - top_score), 0.0)
    row_total = lax.optimization_barrier(jnp.sum(raised, -1, keepdims=True))
    return raised / jnp.where(query_mask, row_total, 1.0)

def gather_blocks(rows, plan):
    blocks_win = rows.shape[0] // BLK
    shaped = rows.reshape((blocks_win, BLK) + rows.shape[1:])[plan]
    return shaped.reshape((blocks_win, KB * BLK) + rows.shape[1:])

def window_forward(queries, key_rows, value_rows, live_rows, plan, head_dim):
    blocks_win = WIN // BLK
    heads_here = queries.shape[1]
    query_blocks = queries.reshape(blocks_win, BLK, heads_here, head_dim)
    key_sel = gather_blocks(key_rows, plan)
    value_sel = gather_blocks(value_rows, plan)
    live_sel = gather_blocks(live_rows, plan)
    query_live = live_rows.reshape(blocks_win, BLK)
    attn_probs = window_probs(query_blocks, key_sel, live_sel, query_live, head_dim ** (-0.5))
    probs_low = attn_probs.astype(jnp.bfloat16)
    context = jnp.einsum('bhqk,bkhd->bqhd', probs_low.astype(jnp.float32), value_sel.astype(jnp.float32))
    return context.astype(jnp.bfloat16).reshape(WIN, heads_here * head_dim)

def window_backward(queries, key_rows, value_rows, live_rows, plan, grad_ctx, head_dim):
    blocks_win = WIN // BLK
    heads_here = queries.shape[1]
    query_blocks = queries.reshape(blocks_win, BLK, heads_here, head_dim)
    key_sel = gather_blocks(key_rows, plan)
    value_sel = gather_blocks(value_rows, plan)
    live_sel = gather_blocks(live_rows, plan)
    query_live = live_rows.reshape(blocks_win, BLK)
    scale = head_dim ** (-0.5)
    attn_probs = window_probs(query_blocks, key_sel, live_sel, query_live, scale)
    probs_low = attn_probs.astype(jnp.bfloat16).astype(jnp.float32)
    grad_blocks = grad_ctx.reshape(blocks_win, BLK, heads_here, head_dim).astype(jnp.float32)
    grad_probs = jnp.einsum('bqhd,bkhd->bhqk', grad_blocks, value_sel.astype(jnp.float32))
    grad_value_sel = jnp.einsum('bhqk,bqhd->bkhd', probs_low, grad_blocks)
    delta = lax.optimization_barrier(jnp.sum(attn_probs * grad_probs, -1, keepdims=True))
    grad_scores = (attn_probs * (grad_probs - delta) * scale).astype(jnp.bfloat16).astype(jnp.float32)
    grad_query = jnp.einsum('bhqk,bkhd->bqhd', grad_scores, key_sel.astype(jnp.float32)).astype(jnp.bfloat16)
    grad_key_sel = jnp.einsum('bhqk,bqhd->bkhd', grad_scores, query_blocks.astype(jnp.float32))
    flat_plan = plan.reshape(-1)
    zeros_win = jnp.zeros((blocks_win, BLK, heads_here, head_dim), jnp.float32)
    grad_key = zeros_win.at[flat_plan].add(grad_key_sel.reshape(blocks_win * KB, BLK, heads_here, head_dim))
    grad_value = zeros_win.at[flat_plan].add(grad_value_sel.reshape(blocks_win * KB, BLK, heads_here, head_dim))
    stacked = jnp.stack([grad_query, grad_key.astype(jnp.bfloat16), grad_value.astype(jnp.bfloat16)], 1)
    return stacked.reshape(WIN, 3, heads_here * head_dim)

def window_plans(pattern, total_windows):
    blocks_win = WIN // BLK
    local_window = jnp.arange(total_windows, dtype=jnp.int32) % (SLOTS // WIN)
    return (pattern.reshape(total_windows, blocks_win, KB) - (local_window * blocks_win)[:, None, None]).astype(jnp.int32)

def reference(points, destination, pattern, norm_gain, qkv_weight, out_weight, grad_out):
    head_dim = D // HEADS
    group_width = D // N_TP
    target = destination[:, 0].reshape(N_PTS, P_DEV)
    owners = jnp.arange(N_PTS, dtype=jnp.int32)
    onehot = (target[:, :, None] == owners[None, None, :]).astype(jnp.int32)
    slot_rank = (lax.optimization_barrier(jnp.sum(jnp.cumsum(onehot, 1).astype(jnp.int32) * onehot, -1)) - 1).astype(jnp.int32)
    slot = (target * SLOTS + owners[:, None] * C_SEND + slot_rank).reshape(-1).astype(jnp.int32)
    total_slots = N_PTS * SLOTS
    live = jnp.zeros((total_slots,), jnp.int32).at[slot].set(1) > 0
    normed, x_hat, inv_std = norm_forward(points, norm_gain)
    qkv_rows = jnp.stack([jnp.dot(normed, qkv_weight[which], preferred_element_type=jnp.float32).astype(jnp.bfloat16) for which in range(3)], 1)
    qkv_slots = jnp.zeros((total_slots, 3, D), jnp.bfloat16).at[slot].set(qkv_rows)
    total_windows = total_slots // WIN
    plans = window_plans(pattern, total_windows)
    split = qkv_slots.reshape(total_windows, WIN, 3, HEADS, head_dim)
    live_win = live.reshape(total_windows, WIN)

    def forward_one(item):
        block_rows, live_rows, plan = item
        return window_forward(block_rows[:, 0], block_rows[:, 1], block_rows[:, 2], live_rows, plan, head_dim)
    context_slots = lax.map(forward_one, (split, live_win, plans)).reshape(total_slots, D)
    context = context_slots[slot]
    total = jnp.zeros((POINTS, D), jnp.float32)
    for group in range(N_TP):
        cols = slice(group * group_width, (group + 1) * group_width)
        part = jnp.dot(context[:, cols], out_weight[cols], preferred_element_type=jnp.float32).astype(jnp.bfloat16)
        total = total + lax.optimization_barrier(part).astype(jnp.float32)
    update = total.astype(jnp.bfloat16)
    out = (points.astype(jnp.float32) + update.astype(jnp.float32)).astype(jnp.bfloat16)
    grad_context = jnp.dot(grad_out, out_weight.T, preferred_element_type=jnp.float32).astype(jnp.bfloat16)
    grad_proj = jnp.dot(context.T, grad_out, preferred_element_type=jnp.float32)
    grad_context_slots = jnp.zeros((total_slots, D), jnp.bfloat16).at[slot].set(grad_context)
    grad_win = grad_context_slots.reshape(total_windows, WIN, HEADS, head_dim)

    def backward_one(item):
        block_rows, live_rows, plan, grad_rows = item
        return window_backward(block_rows[:, 0], block_rows[:, 1], block_rows[:, 2], live_rows, plan, grad_rows, head_dim)
    grad_qkv_slots = lax.map(backward_one, (split, live_win, plans, grad_win)).reshape(total_slots, 3, D)
    grad_qkv_rows = grad_qkv_slots[slot]
    total = jnp.zeros((POINTS, D), jnp.float32)
    for group in range(N_TP):
        cols = slice(group * group_width, (group + 1) * group_width)
        part = jnp.zeros((POINTS, D), jnp.float32)
        for which in range(3):
            part = part + jnp.dot(grad_qkv_rows[:, which, cols], qkv_weight[which][:, cols].T, preferred_element_type=jnp.float32)
        total = total + lax.optimization_barrier(part.astype(jnp.bfloat16)).astype(jnp.float32)
    grad_normed = total.astype(jnp.bfloat16)
    grad_branch, grad_gain = norm_backward(grad_normed, x_hat, inv_std, norm_gain)
    grad_input = (grad_out.astype(jnp.float32) + grad_branch.astype(jnp.float32)).astype(jnp.bfloat16)
    grad_qkv = jnp.stack([jnp.dot(normed.T, grad_qkv_rows[:, which], preferred_element_type=jnp.float32) for which in range(3)], 0)
    return (out, grad_input, grad_qkv, grad_proj, grad_gain)
```

```python
import functools

import jax
import jax.numpy as jnp
from jax import lax
from jax.experimental import pallas as pl
from jax.experimental.pallas import tpu as pltpu
from jax.sharding import PartitionSpec as P

MESH = pl.DeviceIdType.MESH
F32 = jnp.float32
BF16 = jnp.bfloat16
BLK = 128
NBLK = 8
KB = 4
LANES = 128
HALF = 64
EMPTY = 30000.0
EMPTY_CUT = 10000.0
LOW = -1e30


def nn(a, b):
    return jnp.dot(a, b, preferred_element_type=F32)


def nt(a, b):
    return lax.dot_general(a, b, (((1,), (1,)), ((), ())), preferred_element_type=F32)


def wait_bytes(ref, sem):
    pltpu.make_async_copy(ref, ref, sem).wait()


def kernel(
    n,
    tp,
    pts_ref,
    dest_ref,
    pat_ref,
    gain_ref,
    wqkv_ref,
    wo_ref,
    gout_ref,
    out_ref,
    gin_ref,
    gqkv_ref,
    gproj_ref,
    ggain_ref,
    xhat,
    inv_std,
    normed,
    normed_t,
    gout_t,
    pick,
    rows4,
    a_send,
    a_recv,
    qs,
    gs,
    k_t,
    v_t,
    bias,
    probs,
    dscore,
    stack,
    ra_send,
    ra_recv,
    rb_send,
    rb_recv,
    u_send,
    u_recv,
    n_send,
    n_recv,
    o_all,
    i_all,
    gp_send,
    gp_recv,
    gp_all,
    gw_send,
    gw_recv,
    gw_all,
    gg_recv,
    gx_recv,
    ssem,
    rsem,
):
    me = lax.axis_index("pts")
    tm = lax.axis_index("tp")
    cap = a_send.shape[1]
    per_blk = BLK // cap
    group = me // per_blk
    points = pts_ref.shape[0]
    width = pts_ref.shape[1]
    slots = n * cap
    chunk = points // tp

    def remote(src, dst, phase, peer):
        return pltpu.make_async_remote_copy(
            src_ref=src,
            dst_ref=dst,
            send_sem=ssem.at[phase],
            recv_sem=rsem.at[phase],
            device_id=peer,
            device_id_type=MESH,
        )

    def to_pts(send, recv, phase):
        def one(i, carry):
            peer = lax.rem(me + i, n)
            remote(send(peer), recv.at[me], phase, (peer, tm)).start()
            return carry

        lax.fori_loop(1, n, one, 0)

    def to_tp(send, recv, phase):
        for i in range(1, tp):
            peer = lax.rem(tm + i, tp)
            remote(send(peer), recv.at[tm], phase, (me, peer)).start()

    barrier = pltpu.get_barrier_semaphore()

    def greet(i, carry):
        pl.semaphore_signal(
            barrier, inc=1, device_id=(lax.rem(me + i, n), tm), device_id_type=MESH
        )
        return carry

    lax.fori_loop(1, n, greet, 0)
    for i in range(1, tp):
        pl.semaphore_signal(
            barrier, inc=1, device_id=(me, lax.rem(tm + i, tp)), device_id_type=MESH
        )

    def norm(r, carry):
        at = pl.ds(pl.multiple_of(r * BLK, BLK), BLK)
        x = pts_ref[at, :].astype(F32)
        shifted = x - jnp.mean(x, -1, keepdims=True)
        inv = lax.rsqrt(jnp.mean(shifted * shifted, -1, keepdims=True) + 1e-05)
        hat = shifted * inv
        xhat[at, :] = hat
        inv_std[at, :] = inv
        normed[at, :] = (hat * gain_ref[...]).astype(BF16)
        return carry

    lax.fori_loop(0, points // BLK, norm, 0)
    nm = normed[...]
    rows4[:, 0:LANES] = (nn(nm, wqkv_ref[0]).astype(BF16).astype(F32) * 0.125).astype(BF16)
    rows4[:, LANES : 2 * LANES] = nn(nm, wqkv_ref[1]).astype(BF16)
    rows4[:, 2 * LANES : 3 * LANES] = nn(nm, wqkv_ref[2]).astype(BF16)
    rows4[:, 3 * LANES : 4 * LANES] = nt(gout_ref[...], wo_ref[...]).astype(BF16)

    dest = dest_ref[...].astype(F32)
    lane = lax.broadcasted_iota(jnp.int32, (points, LANES), 1).astype(F32)
    onehot = jnp.where(dest == lane, 1.0, 0.0)
    upto = jnp.where(
        lax.broadcasted_iota(jnp.int32, (points, points), 0)
        >= lax.broadcasted_iota(jnp.int32, (points, points), 1),
        1.0,
        0.0,
    ).astype(BF16)
    count = nn(upto, onehot.astype(BF16))
    index = dest * cap + jnp.sum(count * onehot, -1, keepdims=True) - 1.0
    slot_lane = lax.broadcasted_iota(jnp.int32, (points, slots), 1).astype(F32)
    pick[...] = jnp.where(index == slot_lane, 1.0, 0.0).astype(BF16)
    index_row = jnp.broadcast_to(index, (points, LANES)).T[0:1, :]
    slot_sub = lax.broadcasted_iota(jnp.int32, (BLK, points), 0).astype(F32)
    ones = jnp.ones((points, LANES), BF16)

    pl.semaphore_wait(barrier, n - 1 + tp - 1)

    def place(i, carry):
        c = lax.rem(group + i, NBLK)
        base = (c * BLK).astype(F32)
        put = jnp.where(slot_sub + base == index_row, 1.0, 0.0).astype(BF16)
        live = nn(put, ones)
        qkv = nn(put, rows4[:, 0 : 3 * LANES]).astype(BF16)
        g = jnp.where(live > 0.5, nn(put, rows4[:, 3 * LANES : 4 * LANES]), EMPTY).astype(BF16)
        at = pl.ds(c * per_blk, per_blk)
        a_send[at, :, 0 : 3 * LANES] = qkv.reshape(per_blk, cap, 3 * LANES)
        a_send[at, :, 3 * LANES : 4 * LANES] = g.reshape(per_blk, cap, LANES)
        for u in range(per_blk):
            peer = c * per_blk + u

            @pl.when(peer != me)
            def _():
                remote(a_send.at[peer], a_recv.at[me], 0, (peer, tm)).start()

        return carry

    lax.fori_loop(0, NBLK, place, 0)
    a_recv[me] = a_send[me]

    normed_t[...] = nm.astype(F32).T.astype(BF16)
    gout_t[...] = gout_ref[...].astype(F32).T.astype(BF16)
    probs[:, KB] = jnp.zeros((NBLK, BLK, 2 * BLK), BF16)
    dscore[:, KB] = jnp.zeros((NBLK, BLK, 2 * BLK), BF16)

    wait_bytes(a_recv.at[pl.ds(0, n - 1)], rsem.at[0])

    head_lane = lax.broadcasted_iota(jnp.int32, (BLK, LANES), 1) < HALF

    def prepare(b, carry):
        block = a_recv[pl.ds(b * per_blk, per_blk)].reshape(BLK, 4 * LANES)
        q = block[:, 0:LANES].astype(F32)
        g = block[:, 3 * LANES : 4 * LANES].astype(F32)
        empty = g > EMPTY_CUT
        bias[b] = jnp.where(empty, LOW, 0.0)
        g = jnp.where(empty, 0.0, g)
        qs[b, 0:BLK] = jnp.where(head_lane, q, 0.0).astype(BF16)
        qs[b, BLK : 2 * BLK] = jnp.where(head_lane, 0.0, q).astype(BF16)
        gs[b, 0:BLK] = jnp.where(head_lane, g, 0.0).astype(BF16)
        gs[b, BLK : 2 * BLK] = jnp.where(head_lane, 0.0, g).astype(BF16)
        k_t[b] = block[:, LANES : 2 * LANES].astype(F32).T.astype(BF16)
        v_t[b] = block[:, 2 * LANES : 3 * LANES].astype(F32).T.astype(BF16)
        return carry

    lax.fori_loop(0, NBLK, prepare, 0)

    head_sub = lax.broadcasted_iota(jnp.int32, (LANES, BLK), 0) < HALF

    def send_back(send, recv, phase, b, which):
        for u in which:
            peer = b * per_blk + u

            @pl.when(peer != me)
            def _():
                remote(send.at[peer], recv.at[me], phase, (peer, tm)).start()

    def interleave(b, first, count):
        for j in range(3):
            some = stack[b, pl.ds(3 * cap * first + j, cap * count, stride=3), :]
            rb_send[pl.ds(b * per_blk + first, count), :, j * LANES : (j + 1) * LANES] = (
                some.astype(BF16).reshape(count, cap, LANES)
            )

    def attend(i, carry):
        b = lax.rem(group + i, NBLK)
        chosen = [pat_ref[b, j] for j in range(KB)]

        def keyed(first):
            return jnp.concatenate(
                [
                    a_recv[pl.ds(c * per_blk, per_blk), :, first : first + LANES].reshape(
                        BLK, LANES
                    )
                    for c in chosen
                ],
                0,
            )

        low = jnp.concatenate([bias[c] for c in chosen], 0)
        scores = nt(keyed(LANES), qs[b]) + jnp.concatenate([low, low], 1)
        raised = jnp.exp(scores - jnp.max(scores, 0, keepdims=True))
        p = raised * (1.0 / jnp.sum(raised, 0, keepdims=True))
        dp = nt(keyed(2 * LANES), gs[b])
        delta = jnp.sum(p * dp, 0, keepdims=True)
        ds = (p * (dp - delta)).astype(BF16)
        pb = p.astype(BF16)
        probs[b, 0:KB] = pb.reshape(KB, BLK, 2 * BLK)
        dscore[b, 0:KB] = ds.reshape(KB, BLK, 2 * BLK)
        ctx_t = nn(jnp.concatenate([v_t[c] for c in chosen], 1), pb)
        gq_t = nn(jnp.concatenate([k_t[c] for c in chosen], 1), ds)
        ctx = jnp.where(head_sub, ctx_t[:, 0:BLK], ctx_t[:, BLK : 2 * BLK]).T
        gq = jnp.where(head_sub, gq_t[:, 0:BLK], gq_t[:, BLK : 2 * BLK]).T * 0.125
        at = pl.ds(b * per_blk, per_blk)
        ra_send[at] = ctx.astype(BF16).reshape(per_blk, cap, LANES)
        send_back(ra_send, ra_recv, 1, b, range(per_blk))
        stack[b, 0:BLK] = gq
        interleave(b, 0, 1)
        send_back(rb_send, rb_recv, 2, b, range(1))
        return carry

    lax.fori_loop(0, NBLK, attend, 0)
    ra_recv[me] = ra_send[me]

    def attend_keys(i, carry):
        c = lax.rem(group + i, NBLK)
        gk = jnp.zeros((BLK, LANES), F32)
        gv = jnp.zeros((BLK, LANES), F32)
        for b in range(NBLK):
            j = jnp.int32(KB)
            for which in range(KB):
                j = jnp.where(pat_ref[b, which] == c, which, j)
            gk = gk + nn(dscore[b, j], qs[b])
            gv = gv + nn(probs[b, j], gs[b])
        stack[c, BLK : 2 * BLK] = gk
        stack[c, 2 * BLK : 3 * BLK] = gv
        interleave(c, 1, per_blk - 1)
        send_back(rb_send, rb_recv, 2, c, range(1, per_blk))
        return carry

    lax.fori_loop(0, NBLK, attend_keys, 0)
    rb_recv[me] = rb_send[me]

    wait_bytes(ra_recv.at[pl.ds(0, n - 1)], rsem.at[1])
    context = nn(pick[...], ra_recv[...].reshape(slots, LANES)).astype(BF16)
    u_send[...] = nn(context, wo_ref[...]).astype(BF16).reshape(tp, chunk, width)
    to_tp(lambda peer: u_send.at[peer], u_recv, 3)
    gp_send[...] = nn(gout_t[...], context).astype(BF16).reshape(gp_send.shape)
    to_pts(lambda peer: gp_send.at[peer], gp_recv, 4)

    mine = pl.ds(pl.multiple_of(tm * chunk, chunk), chunk)
    u_recv[tm] = u_send[tm]
    wait_bytes(u_recv.at[pl.ds(0, tp - 1)], rsem.at[3])
    update = jnp.sum(u_recv[...].astype(F32), 0).astype(BF16).astype(F32)
    o_all[tm] = (pts_ref[mine, :].astype(F32) + update).astype(BF16)
    to_tp(lambda peer: o_all.at[tm], o_all, 5)

    gp_recv[me] = gp_send[me]
    wait_bytes(gp_recv.at[pl.ds(0, n - 1)], rsem.at[4])
    gp_all[me] = jnp.sum(gp_recv[...].astype(F32), 0).astype(BF16)
    to_pts(lambda peer: gp_all.at[me], gp_all, 6)

    wait_bytes(rb_recv.at[pl.ds(0, n - 1)], rsem.at[2])
    back = nn(pick[...], rb_recv[...].reshape(slots, 3 * LANES)).astype(BF16)
    gq = back[:, 0:LANES]
    gk = back[:, LANES : 2 * LANES]
    gv = back[:, 2 * LANES : 3 * LANES]
    part = nt(gq, wqkv_ref[0]) + nt(gk, wqkv_ref[1]) + nt(gv, wqkv_ref[2])
    n_send[...] = part.astype(BF16).reshape(tp, chunk, width)
    to_tp(lambda peer: n_send.at[peer], n_recv, 7)
    nmt = normed_t[...]
    grads = jnp.concatenate([nn(nmt, gq), nn(nmt, gk), nn(nmt, gv)], 0)
    gw_send[...] = grads.astype(BF16).reshape(gw_send.shape)
    to_pts(lambda peer: gw_send.at[peer], gw_recv, 8)
    gain_part = jnp.sum(part * xhat[...], 0, keepdims=True)
    for j in range(width // LANES):
        gg_recv[me, j] = gain_part[:, j * LANES : (j + 1) * LANES]
    to_pts(lambda peer: gg_recv.at[me], gg_recv, 9)

    n_recv[tm] = n_send[tm]
    wait_bytes(n_recv.at[pl.ds(0, tp - 1)], rsem.at[7])
    grad = jnp.sum(n_recv[...].astype(F32), 0).astype(BF16).astype(F32)
    hat = xhat[mine, :]
    scaled = grad * gain_ref[...]
    first = jnp.mean(scaled, -1, keepdims=True)
    second = jnp.mean(scaled * hat, -1, keepdims=True)
    branch = (inv_std[mine, :] * (scaled - first - hat * second)).astype(BF16).astype(F32)
    i_all[tm] = (gout_ref[mine, :].astype(F32) + branch).astype(BF16)
    to_tp(lambda peer: i_all.at[tm], i_all, 10)

    gw_recv[me] = gw_send[me]
    wait_bytes(gw_recv.at[pl.ds(0, n - 1)], rsem.at[8])
    gw_all[me] = jnp.sum(gw_recv[...].astype(F32), 0).astype(BF16)
    to_pts(lambda peer: gw_all.at[me], gw_all, 11)

    wait_bytes(gg_recv.at[pl.ds(0, n - 1)], rsem.at[9])
    gx_recv[tm] = jnp.sum(gg_recv[...], 0)
    to_tp(lambda peer: gx_recv.at[tm], gx_recv, 12)

    wait_bytes(o_all.at[pl.ds(0, tp - 1)], rsem.at[5])
    out_ref[...] = o_all[...].reshape(points, width)
    wait_bytes(gp_all.at[pl.ds(0, n - 1)], rsem.at[6])
    proj_t = gp_all[...].reshape(width, LANES).astype(F32)
    gproj_ref[...] = proj_t.T
    wait_bytes(i_all.at[pl.ds(0, tp - 1)], rsem.at[10])
    gin_ref[...] = i_all[...].reshape(points, width)
    wait_bytes(gx_recv.at[pl.ds(0, tp - 1)], rsem.at[12])
    gain_sum = jnp.sum(gx_recv[...], 0)
    for j in range(width // LANES):
        ggain_ref[:, j * LANES : (j + 1) * LANES] = gain_sum[j]
    wait_bytes(gw_all.at[pl.ds(0, n - 1)], rsem.at[11])
    gqkv_ref[...] = gw_all[...].reshape(gqkv_ref.shape).astype(F32)

    pts_bufs = ((0, a_send), (1, ra_send), (2, rb_send), (4, gp_send), (6, gp_all))
    pts_bufs += ((8, gw_send), (9, gg_recv), (11, gw_all))
    for phase, buf in pts_bufs:
        wait_bytes(buf.at[pl.ds(0, n - 1)], ssem.at[phase])
    for phase, buf in ((3, u_send), (5, o_all), (7, n_send), (10, i_all), (12, gx_recv)):
        wait_bytes(buf.at[pl.ds(0, tp - 1)], ssem.at[phase])


def body(n, tp, points, destination, pattern, norm_gain, qkv_weight, out_weight, grad_out):
    rows, width = points.shape
    cap = 2 * rows // n
    slots = n * cap
    chunk = rows // tp
    wrows = 3 * width // n
    prows = width // n
    vm = pl.BlockSpec(memory_space=pltpu.VMEM)
    scratch = [
        pltpu.VMEM((rows, width), F32),
        pltpu.VMEM((rows, 1), F32),
        pltpu.VMEM((rows, width), BF16),
        pltpu.VMEM((width, rows), BF16),
        pltpu.VMEM((width, rows), BF16),
        pltpu.VMEM((rows, slots), BF16),
        pltpu.VMEM((rows, 4 * LANES), BF16),
        pltpu.VMEM((n, cap, 4 * LANES), BF16),
        pltpu.VMEM((n, cap, 4 * LANES), BF16),
        pltpu.VMEM((NBLK, 2 * BLK, LANES), BF16),
        pltpu.VMEM((NBLK, 2 * BLK, LANES), BF16),
        pltpu.VMEM((NBLK, LANES, BLK), BF16),
        pltpu.VMEM((NBLK, LANES, BLK), BF16),
        pltpu.VMEM((NBLK, BLK, LANES), F32),
        pltpu.VMEM((NBLK, KB + 1, BLK, 2 * BLK), BF16),
        pltpu.VMEM((NBLK, KB + 1, BLK, 2 * BLK), BF16),
        pltpu.VMEM((NBLK, 3 * BLK, LANES), F32),
        pltpu.VMEM((n, cap, LANES), BF16),
        pltpu.VMEM((n, cap, LANES), BF16),
        pltpu.VMEM((n, cap, 3 * LANES), BF16),
        pltpu.VMEM((n, cap, 3 * LANES), BF16),
        pltpu.VMEM((tp, chunk, width), BF16),
        pltpu.VMEM((tp, chunk, width), BF16),
        pltpu.VMEM((tp, chunk, width), BF16),
        pltpu.VMEM((tp, chunk, width), BF16),
        pltpu.VMEM((tp, chunk, width), BF16),
        pltpu.VMEM((tp, chunk, width), BF16),
        pltpu.VMEM((n, prows, LANES), BF16),
        pltpu.VMEM((n, prows, LANES), BF16),
        pltpu.VMEM((n, prows, LANES), BF16),
        pltpu.VMEM((n, wrows, LANES), BF16),
        pltpu.VMEM((n, wrows, LANES), BF16),
        pltpu.VMEM((n, wrows, LANES), BF16),
        pltpu.VMEM((n, width // LANES, 1, LANES), F32),
        pltpu.VMEM((tp, width // LANES, 1, LANES), F32),
        pltpu.SemaphoreType.DMA((13,)),
        pltpu.SemaphoreType.DMA((13,)),
    ]
    out, grad_input, grad_qkv, grad_proj, grad_gain = pl.pallas_call(
        functools.partial(kernel, n, tp),
        out_shape=(
            jax.ShapeDtypeStruct((rows, width), BF16),
            jax.ShapeDtypeStruct((rows, width), BF16),
            jax.ShapeDtypeStruct((3, width, LANES), F32),
            jax.ShapeDtypeStruct((LANES, width), F32),
            jax.ShapeDtypeStruct((1, width), F32),
        ),
        in_specs=[vm, vm, pl.BlockSpec(memory_space=pltpu.SMEM), vm, vm, vm, vm],
        out_specs=(vm,) * 5,
        scratch_shapes=scratch,
        compiler_params=pltpu.CompilerParams(
            collective_id=0, has_side_effects=True, vmem_limit_bytes=48 * 1024 * 1024
        ),
        name="point_attention",
    )(
        points,
        destination,
        pattern,
        norm_gain.reshape(1, width),
        qkv_weight,
        out_weight,
        grad_out,
    )
    return out, grad_input, grad_qkv, grad_proj, grad_gain.reshape(width)


def solution(mesh):
    return jax.shard_map(
        functools.partial(body, mesh.shape["pts"], mesh.shape["tp"]),
        mesh=mesh,
        in_specs=(
            P("pts", None),
            P("pts", None),
            P("pts", None),
            P(),
            P(None, None, "tp"),
            P("tp", None),
            P("pts", None),
        ),
        out_specs=(P("pts", None), P("pts", None), P(None, None, "tp"), P("tp", None), P()),
        check_vma=False,
    )
```

```python
import functools

import jax
import jax.numpy as jnp
from jax import lax
from jax.experimental import pallas as pl
from jax.experimental.pallas import tpu as pltpu
from jax.sharding import PartitionSpec as P

MESH = pl.DeviceIdType.MESH
F32 = jnp.float32
BF16 = jnp.bfloat16
BLK = 128
NBLK = 8
KB = 4
LANES = 128
HALF = 64
EMPTY = 2e38
EMPTY_CUT = 1e38
LOW = -1e30
VMEM_LIMIT = 60 * 1024 * 1024
YS, ZS, CORES = 4, 4, 2


def ring(step, size):
    return min(step, size - step)


OFFSETS = sorted(
    [(y, z, c) for y in range(YS) for z in range(ZS) for c in range(CORES)][1:],
    key=lambda o: (-ring(o[0], YS) - ring(o[1], ZS), o),
)

(K_Q, K_V, K_G, K_CTX, K_BACK, K_UPD, K_OUT, K_N0, K_N1, K_I0, K_I1, K_W, K_WALL, K_GAIN, K_GAINX) = (
    range(15)
)


def nn(a, b):
    return jnp.dot(a, b, preferred_element_type=F32)


def nt(a, b):
    return lax.dot_general(a, b, (((1,), (1,)), ((), ())), preferred_element_type=F32)


def wait_bytes(ref, sem):
    pltpu.make_async_copy(ref, ref, sem).wait()


def kernel(
    n,
    tp,
    pts_hbm,
    dest_hbm,
    pat_hbm,
    gain_hbm,
    wqkv_hbm,
    wo_hbm,
    gout_hbm,
    out_ref,
    gin_ref,
    gqkv_ref,
    gproj_ref,
    ggain_ref,
    pts_ref,
    dest_ref,
    pat_ref,
    gain_ref,
    wqkv_ref,
    wo_ref,
    gout_ref,
    in_sem,
    xhat,
    inv_std,
    normed,
    normed_t,
    gout_t,
    pick,
    put_all,
    rows_kq,
    rows_vg,
    kq_send,
    kq_recv,
    v_send,
    v_recv,
    g_send,
    g_recv,
    qs,
    gs,
    k_t,
    v_t,
    bias,
    probs,
    gk_part,
    gv_part,
    stack,
    ra_send,
    ra_recv,
    rb_send,
    rb_recv,
    u_send,
    u_recv,
    n_send,
    n_recv,
    o_all,
    i_all,
    gw_send,
    gw_recv,
    gw_all,
    gg_recv,
    gx_recv,
    ssem,
    rsem,
):
    me = lax.axis_index("pts")
    tm = lax.axis_index("tp")
    cap = kq_send.shape[1]
    per_blk = BLK // cap
    points, width = pts_ref.shape
    slots = n * cap
    chunk = points // tp
    half = chunk // 2
    my_y = me // (ZS * CORES)
    my_z = lax.rem(me // CORES, ZS)
    my_c = lax.rem(me, CORES)

    barrier = pltpu.get_barrier_semaphore()

    def greet(i, carry):
        pl.semaphore_signal(
            barrier, inc=1, device_id=(lax.rem(me + i, n), tm), device_id_type=MESH
        )
        return carry

    for i in range(1, tp):
        pl.semaphore_signal(
            barrier, inc=1, device_id=(me, lax.rem(tm + i, tp)), device_id_type=MESH
        )
    lax.fori_loop(1, n, greet, 0)

    fetches = [
        pltpu.make_async_copy(src, dst, in_sem.at[i])
        for i, (src, dst) in enumerate(
            (
                (dest_hbm, dest_ref),
                (pts_hbm, pts_ref),
                (gain_hbm, gain_ref),
                (wqkv_hbm, wqkv_ref),
                (gout_hbm, gout_ref),
                (wo_hbm, wo_ref),
                (pat_hbm, pat_ref),
            )
        )
    ]
    for fetch in fetches:
        fetch.start()

    def remote(src, dst, phase, peer):
        return pltpu.make_async_remote_copy(
            src_ref=src,
            dst_ref=dst,
            send_sem=ssem.at[phase],
            recv_sem=rsem.at[phase],
            device_id=peer,
            device_id_type=MESH,
        )

    def to_pts(send, recv, phase):
        for dy, dz, dc in OFFSETS:
            peer = (lax.rem(my_y + dy, YS) * ZS + lax.rem(my_z + dz, ZS)) * CORES
            peer = peer + lax.rem(my_c + dc, CORES)
            remote(send(peer), recv.at[me], phase, (peer, tm)).start()

    def to_tp(send, recv, phase):
        for i in range(1, tp):
            peer = lax.rem(tm + i, tp)
            remote(send(peer), recv(tm), phase, (me, peer)).start()

    def nth(i):
        dy = jnp.where(i < 2, 2, jnp.where(i < 6, 1 + 2 * lax.rem(i, 2), 0))
        dz = jnp.where(i < 2, 1 - i, jnp.where(i < 6, 1 - (i - 2) // 2, 7 - i))
        return lax.rem(my_y + dy, YS) * 2 + lax.rem(my_z // 2 + dz, 2)

    def to_group(send, recv, phase, b, which):
        for u in which:
            peer = b * per_blk + u

            @pl.when(peer != me)
            def _():
                remote(send.at[peer], recv.at[me], phase, (peer, tm)).start()

    upto = jnp.where(
        lax.broadcasted_iota(jnp.int32, (points, points), 0)
        <= lax.broadcasted_iota(jnp.int32, (points, points), 1),
        1.0,
        0.0,
    ).astype(BF16)
    fetches[0].wait()
    dest = dest_ref[...].astype(F32)
    owner = lax.broadcasted_iota(jnp.int32, (n, points), 0).astype(F32)
    onehot = jnp.where(dest == owner, 1.0, 0.0)
    count = nn(onehot.astype(BF16), upto)
    index = dest * cap + jnp.sum(count * onehot, 0, keepdims=True) - 1.0

    fetches[1].wait()
    fetches[2].wait()

    def norm(r, carry):
        at = pl.ds(pl.multiple_of(r * BLK, BLK), BLK)
        x = pts_ref[at, :].astype(F32)
        shifted = x - jnp.mean(x, -1, keepdims=True)
        inv = lax.rsqrt(jnp.mean(shifted * shifted, -1, keepdims=True) + 1e-05)
        hat = shifted * inv
        xhat[at, :] = hat
        inv_std[at, :] = inv
        normed[at, :] = (hat * gain_ref[...]).astype(BF16)
        return carry

    lax.fori_loop(0, points // BLK, norm, 0)
    fetches[3].wait()
    nm = normed[...]
    rows_kq[:, 0:LANES] = nn(nm, wqkv_ref[1]).astype(BF16)
    rows_kq[:, LANES : 2 * LANES] = (nn(nm, wqkv_ref[0]).astype(BF16).astype(F32) * 0.125).astype(
        BF16
    )
    slot_sub = lax.broadcasted_iota(jnp.int32, (BLK, points), 0).astype(F32)
    ones = jnp.ones((points, LANES), BF16)

    pl.semaphore_wait(barrier, n - 1 + tp - 1)

    def place(i, carry):
        c = nth(i)
        base = (c * BLK).astype(F32)
        put = jnp.where(slot_sub + base == index, 1.0, 0.0).astype(BF16)
        put_all[c] = put
        live = nn(put, ones)
        kq = nn(put, rows_kq[...])
        k = kq[:, 0:LANES].astype(BF16)
        q = jnp.where(live > 0.5, kq[:, LANES : 2 * LANES], EMPTY).astype(BF16)
        at = pl.ds(c * per_blk, per_blk)
        kq_send[at, :, 0:LANES] = k.reshape(per_blk, cap, LANES)
        kq_send[at, :, LANES : 2 * LANES] = q.reshape(per_blk, cap, LANES)
        to_group(kq_send, kq_recv, K_Q, c, range(per_blk))
        return carry

    lax.fori_loop(0, NBLK, place, 0)
    kq_recv[me] = kq_send[me]

    fetches[4].wait()
    fetches[5].wait()
    rows_vg[:, 0:LANES] = nn(nm, wqkv_ref[2]).astype(BF16)
    rows_vg[:, LANES : 2 * LANES] = nt(gout_ref[...], wo_ref[...]).astype(BF16)

    def place_more(i, carry):
        c = nth(i)
        vg = nn(put_all[c], rows_vg[...]).astype(BF16)
        at = pl.ds(c * per_blk, per_blk)
        v_send[at] = vg[:, 0:LANES].reshape(per_blk, cap, LANES)
        g_send[at] = vg[:, LANES : 2 * LANES].reshape(per_blk, cap, LANES)
        to_group(v_send, v_recv, K_V, c, range(per_blk))
        return carry

    lax.fori_loop(0, NBLK, place_more, 0)
    to_pts(lambda peer: g_send.at[peer], g_recv, K_G)
    v_recv[me] = v_send[me]
    g_recv[me] = g_send[me]

    fetches[6].wait()
    index_col = jnp.broadcast_to(index, (LANES, points)).T
    lane = lax.broadcasted_iota(jnp.int32, (points, LANES), 1).astype(F32)
    for t in range(slots // LANES):
        pick[:, t * LANES : (t + 1) * LANES] = jnp.where(
            index_col == lane + t * LANES, 1.0, 0.0
        ).astype(BF16)
    normed_t[...] = nm.astype(F32).T.astype(BF16)
    gout_t[...] = gout_ref[...].astype(F32).T.astype(BF16)
    gk_part[:, KB] = jnp.zeros((NBLK, BLK, LANES), F32)
    gv_part[:, KB] = jnp.zeros((NBLK, BLK, LANES), F32)

    head_lane = lax.broadcasted_iota(jnp.int32, (BLK, LANES), 1) < HALF
    head_sub = lax.broadcasted_iota(jnp.int32, (LANES, BLK), 0) < HALF

    def block_of(ref, b, first=0):
        return ref[pl.ds(b * per_blk, per_blk), :, first : first + LANES].reshape(BLK, LANES)

    def halves(ref, b, rows):
        ref[b, 0:BLK] = jnp.where(head_lane, rows, 0.0).astype(BF16)
        ref[b, BLK : 2 * BLK] = jnp.where(head_lane, 0.0, rows).astype(BF16)

    def chosen_of(b):
        return [pat_ref[j, b] for j in range(KB)]

    wait_bytes(kq_recv.at[pl.ds(0, n - 1)], rsem.at[K_Q])

    def prepare(b, carry):
        q = block_of(kq_recv, b, LANES).astype(F32)
        empty = q > EMPTY_CUT
        bias[b] = jnp.where(empty, LOW, 0.0)
        halves(qs, b, jnp.where(empty, 0.0, q))
        k_t[b] = block_of(kq_recv, b).astype(F32).T.astype(BF16)
        return carry

    lax.fori_loop(0, NBLK, prepare, 0)

    def softmax(b, carry):
        chosen = chosen_of(b)
        keys = jnp.concatenate([block_of(kq_recv, c) for c in chosen], 0)
        low = jnp.concatenate([bias[c] for c in chosen], 0)
        scores = nt(keys, qs[b]) + jnp.concatenate([low, low], 1)
        raised = jnp.exp(scores - jnp.max(scores, 0, keepdims=True))
        p = raised * (1.0 / jnp.sum(raised, 0, keepdims=True))
        probs[b] = p.astype(BF16)
        return carry

    lax.fori_loop(0, NBLK, softmax, 0)

    wait_bytes(v_recv.at[pl.ds(0, n - 1)], rsem.at[K_V])

    def prepare_v(b, carry):
        v_t[b] = block_of(v_recv, b).astype(F32).T.astype(BF16)
        return carry

    lax.fori_loop(0, NBLK, prepare_v, 0)

    def mix(i, carry):
        b = nth(i)
        values_t = jnp.concatenate([v_t[c] for c in chosen_of(b)], 1)
        ctx_t = nn(values_t, probs[b])
        ctx = jnp.where(head_sub, ctx_t[:, 0:BLK], ctx_t[:, BLK : 2 * BLK]).T
        at = pl.ds(b * per_blk, per_blk)
        ra_send[at] = ctx.astype(BF16).reshape(per_blk, cap, LANES)
        to_group(ra_send, ra_recv, K_CTX, b, range(per_blk))
        return carry

    lax.fori_loop(0, NBLK, mix, 0)
    ra_recv[me] = ra_send[me]

    wait_bytes(g_recv.at[pl.ds(0, n - 1)], rsem.at[K_G])

    def prepare_g(b, carry):
        halves(gs, b, block_of(g_recv, b).astype(F32))
        return carry

    lax.fori_loop(0, NBLK, prepare_g, 0)

    def interleave(b, first, count):
        for j in range(3):
            some = stack[b, pl.ds(3 * cap * first + j, cap * count, stride=3), :]
            rb_send[pl.ds(b * per_blk + first, count), :, j * LANES : (j + 1) * LANES] = (
                some.astype(BF16).reshape(count, cap, LANES)
            )

    def grads_of(i, carry):
        b = nth(i)
        chosen = chosen_of(b)
        pb = probs[b]
        p = pb.astype(F32)
        dp = nt(jnp.concatenate([block_of(v_recv, c) for c in chosen], 0), gs[b])
        delta = jnp.sum(p * dp, 0, keepdims=True)
        ds = (p * (dp - delta)).astype(BF16)
        gq_t = nn(jnp.concatenate([k_t[c] for c in chosen], 1), ds)
        gk_part[b, 0:KB] = nn(ds, qs[b]).reshape(KB, BLK, LANES)
        gv_part[b, 0:KB] = nn(pb, gs[b]).reshape(KB, BLK, LANES)
        gq = jnp.where(head_sub, gq_t[:, 0:BLK], gq_t[:, BLK : 2 * BLK]).T * 0.125
        stack[b, 0:BLK] = gq
        interleave(b, 0, 1)
        to_group(rb_send, rb_recv, K_BACK, b, range(1))
        return carry

    lax.fori_loop(0, NBLK, grads_of, 0)

    def key_side(i, carry):
        c = nth(i)
        gk = jnp.zeros((BLK, LANES), F32)
        gv = jnp.zeros((BLK, LANES), F32)
        for b in range(NBLK):
            j = jnp.int32(KB)
            for which in range(KB):
                j = jnp.where(pat_ref[which, b] == c, which, j)
            gk = gk + gk_part[b, j]
            gv = gv + gv_part[b, j]
        stack[c, BLK : 2 * BLK] = gk
        stack[c, 2 * BLK : 3 * BLK] = gv
        interleave(c, 1, per_blk - 1)
        to_group(rb_send, rb_recv, K_BACK, c, range(1, per_blk))
        return carry

    lax.fori_loop(0, NBLK, key_side, 0)
    rb_recv[me] = rb_send[me]

    wait_bytes(ra_recv.at[pl.ds(0, n - 1)], rsem.at[K_CTX])
    context = nn(pick[...], ra_recv[...].reshape(slots, LANES)).astype(BF16)
    u_send[...] = nn(context, wo_ref[...]).astype(BF16).reshape(tp, chunk, width)
    to_tp(lambda peer: u_send.at[peer], lambda at: u_recv.at[at], K_UPD)
    qkv_rows = 3 * width // n
    proj = nn(gout_t[...], context).astype(BF16)
    gw_send[:, qkv_rows:] = proj.reshape(n, width // n, LANES)

    mine = pl.ds(pl.multiple_of(tm * chunk, chunk), chunk)
    u_recv[tm] = u_send[tm]
    wait_bytes(u_recv.at[pl.ds(0, tp - 1)], rsem.at[K_UPD])
    update = jnp.sum(u_recv[...].astype(F32), 0).astype(BF16).astype(F32)
    o_all[tm] = (pts_ref[mine, :].astype(F32) + update).astype(BF16)
    to_tp(lambda peer: o_all.at[tm], lambda at: o_all.at[at], K_OUT)

    wait_bytes(rb_recv.at[pl.ds(0, n - 1)], rsem.at[K_BACK])
    back = nn(pick[...], rb_recv[...].reshape(slots, 3 * LANES)).astype(BF16)
    gq = back[:, 0:LANES]
    gk = back[:, LANES : 2 * LANES]
    gv = back[:, 2 * LANES : 3 * LANES]
    part = nt(gq, wqkv_ref[0]) + nt(gk, wqkv_ref[1]) + nt(gv, wqkv_ref[2])
    n_send[...] = part.astype(BF16).reshape(tp, chunk, width)
    parts = ((K_N0, K_I0, pl.ds(0, half)), (K_N1, K_I1, pl.ds(half, half)))
    for phase, _, at_half in parts:
        to_tp(
            lambda peer: n_send.at[peer, at_half], lambda at: n_recv.at[at, at_half], phase
        )
    nmt = normed_t[...]
    for j, g in enumerate((gq, gk, gv)):
        gw = nn(nmt, g).astype(BF16)
        for i in range(n):
            first, last = max(i * qkv_rows, j * width), min((i + 1) * qkv_rows, (j + 1) * width)
            if first < last:
                gw_send[i, first - i * qkv_rows : last - i * qkv_rows] = gw[
                    first - j * width : last - j * width
                ]
    to_pts(lambda peer: gw_send.at[peer], gw_recv, K_W)
    gain_part = jnp.sum(part * xhat[...], 0, keepdims=True)
    for j in range(width // LANES):
        gg_recv[me, j] = gain_part[:, j * LANES : (j + 1) * LANES]
    to_pts(lambda peer: gg_recv.at[me], gg_recv, K_GAIN)

    n_recv[tm] = n_send[tm]
    for which, (phase, phase_out, at_half) in enumerate(parts):
        wait_bytes(n_recv.at[pl.ds(0, tp - 1), at_half], rsem.at[phase])
        mine_half = pl.ds(pl.multiple_of(tm * chunk + which * half, half), half)
        grad = jnp.sum(n_recv[:, at_half].astype(F32), 0).astype(BF16).astype(F32)
        hat = xhat[mine_half, :]
        scaled = grad * gain_ref[...]
        first = jnp.mean(scaled, -1, keepdims=True)
        second = jnp.mean(scaled * hat, -1, keepdims=True)
        branch = inv_std[mine_half, :] * (scaled - first - hat * second)
        branch = branch.astype(BF16).astype(F32)
        i_all[tm, at_half] = (gout_ref[mine_half, :].astype(F32) + branch).astype(BF16)
        to_tp(
            lambda peer: i_all.at[tm, at_half], lambda at: i_all.at[at, at_half], phase_out
        )

    gw_recv[me] = gw_send[me]
    wait_bytes(gw_recv.at[pl.ds(0, n - 1)], rsem.at[K_W])
    gw_all[me] = jnp.sum(gw_recv[...].astype(F32), 0).astype(BF16)
    to_pts(lambda peer: gw_all.at[me], gw_all, K_WALL)

    wait_bytes(gg_recv.at[pl.ds(0, n - 1)], rsem.at[K_GAIN])
    gx_recv[tm] = jnp.sum(gg_recv[...], 0)
    to_tp(lambda peer: gx_recv.at[tm], lambda at: gx_recv.at[at], K_GAINX)

    wait_bytes(o_all.at[pl.ds(0, tp - 1)], rsem.at[K_OUT])
    out_ref[...] = o_all[...].reshape(points, width)
    wait_bytes(gw_all.at[pl.ds(0, n - 1)], rsem.at[K_WALL])
    gqkv_ref[...] = gw_all[:, 0:qkv_rows].astype(F32).reshape(gqkv_ref.shape)
    gproj_ref[...] = gw_all[:, qkv_rows:].astype(F32).reshape(width, LANES).T
    wait_bytes(gx_recv.at[pl.ds(0, tp - 1)], rsem.at[K_GAINX])
    gain_sum = jnp.sum(gx_recv[...], 0)
    for j in range(width // LANES):
        ggain_ref[:, j * LANES : (j + 1) * LANES] = gain_sum[j]
    for _, phase_out, at_half in parts:
        wait_bytes(i_all.at[pl.ds(0, tp - 1), at_half], rsem.at[phase_out])
    gin_ref[...] = i_all[...].reshape(points, width)

    for phase, buf in (
        (K_Q, kq_send),
        (K_V, v_send),
        (K_G, g_send),
        (K_CTX, ra_send),
        (K_BACK, rb_send),
        (K_W, gw_send),
        (K_GAIN, gg_recv),
        (K_WALL, gw_all),
    ):
        wait_bytes(buf.at[pl.ds(0, n - 1)], ssem.at[phase])
    for phase, buf in ((K_UPD, u_send), (K_OUT, o_all), (K_GAINX, gx_recv)):
        wait_bytes(buf.at[pl.ds(0, tp - 1)], ssem.at[phase])
    for phase, phase_out, at_half in parts:
        wait_bytes(n_send.at[pl.ds(0, tp - 1), at_half], ssem.at[phase])
        wait_bytes(i_all.at[pl.ds(0, tp - 1), at_half], ssem.at[phase_out])


def hand_out(*refs):
    count = len(refs) // 2
    sems = refs[-1]
    copies = [
        pltpu.make_async_copy(refs[i], refs[count + i], sems.at[i]) for i in range(count)
    ]
    for copy in copies:
        copy.start()
    for copy in copies:
        copy.wait()


def body(n, tp, points, destination, pattern, norm_gain, qkv_weight, out_weight, grad_out):
    rows, width = points.shape
    cap = 2 * rows // n
    slots = n * cap
    chunk = rows // tp
    wrows = 4 * width // n
    vm = pl.BlockSpec(memory_space=pltpu.VMEM)
    hbm = pl.BlockSpec(memory_space=pltpu.HBM)
    any_space = pl.BlockSpec(memory_space=pl.ANY)
    scratch = [
        pltpu.VMEM((rows, width), BF16),
        pltpu.VMEM((1, rows), jnp.int32),
        pltpu.SMEM((KB, NBLK), jnp.int32),
        pltpu.VMEM((1, width), F32),
        pltpu.VMEM((3, width, LANES), BF16),
        pltpu.VMEM((LANES, width), BF16),
        pltpu.VMEM((rows, width), BF16),
        pltpu.SemaphoreType.DMA((7,)),
        pltpu.VMEM((rows, width), F32),
        pltpu.VMEM((rows, 1), F32),
        pltpu.VMEM((rows, width), BF16),
        pltpu.VMEM((width, rows), BF16),
        pltpu.VMEM((width, rows), BF16),
        pltpu.VMEM((rows, slots), BF16),
        pltpu.VMEM((NBLK, BLK, rows), BF16),
        pltpu.VMEM((rows, 2 * LANES), BF16),
        pltpu.VMEM((rows, 2 * LANES), BF16),
        pltpu.VMEM((n, cap, 2 * LANES), BF16),
        pltpu.VMEM((n, cap, 2 * LANES), BF16),
        pltpu.VMEM((n, cap, LANES), BF16),
        pltpu.VMEM((n, cap, LANES), BF16),
        pltpu.VMEM((n, cap, LANES), BF16),
        pltpu.VMEM((n, cap, LANES), BF16),
        pltpu.VMEM((NBLK, 2 * BLK, LANES), BF16),
        pltpu.VMEM((NBLK, 2 * BLK, LANES), BF16),
        pltpu.VMEM((NBLK, LANES, BLK), BF16),
        pltpu.VMEM((NBLK, LANES, BLK), BF16),
        pltpu.VMEM((NBLK, BLK, LANES), F32),
        pltpu.VMEM((NBLK, KB * BLK, 2 * BLK), BF16),
        pltpu.VMEM((NBLK, KB + 1, BLK, LANES), F32),
        pltpu.VMEM((NBLK, KB + 1, BLK, LANES), F32),
        pltpu.VMEM((NBLK, 3 * BLK, LANES), F32),
        pltpu.VMEM((n, cap, LANES), BF16),
        pltpu.VMEM((n, cap, LANES), BF16),
        pltpu.VMEM((n, cap, 3 * LANES), BF16),
        pltpu.VMEM((n, cap, 3 * LANES), BF16),
        pltpu.VMEM((tp, chunk, width), BF16),
        pltpu.VMEM((tp, chunk, width), BF16),
        pltpu.VMEM((tp, chunk, width), BF16),
        pltpu.VMEM((tp, chunk, width), BF16),
        pltpu.VMEM((tp, chunk, width), BF16),
        pltpu.VMEM((tp, chunk, width), BF16),
        pltpu.VMEM((n, wrows, LANES), BF16),
        pltpu.VMEM((n, wrows, LANES), BF16),
        pltpu.VMEM((n, wrows, LANES), BF16),
        pltpu.VMEM((n, width // LANES, 1, LANES), F32),
        pltpu.VMEM((tp, width // LANES, 1, LANES), F32),
        pltpu.SemaphoreType.DMA((15,)),
        pltpu.SemaphoreType.DMA((15,)),
    ]
    shapes = (
        jax.ShapeDtypeStruct((rows, width), BF16),
        jax.ShapeDtypeStruct((rows, width), BF16),
        jax.ShapeDtypeStruct((3, width, LANES), F32),
        jax.ShapeDtypeStruct((LANES, width), F32),
        jax.ShapeDtypeStruct((1, width), F32),
    )
    results = pl.pallas_call(
        functools.partial(kernel, n, tp),
        out_shape=shapes,
        in_specs=[hbm] * 7,
        out_specs=(vm,) * 5,
        scratch_shapes=scratch,
        compiler_params=pltpu.CompilerParams(
            collective_id=0, has_side_effects=True, vmem_limit_bytes=VMEM_LIMIT
        ),
        name="point_attention",
    )(
        points,
        destination.reshape(1, rows),
        pattern.T,
        norm_gain.reshape(1, width),
        qkv_weight,
        out_weight,
        grad_out,
    )
    out, grad_input, grad_qkv, grad_proj, grad_gain = pl.pallas_call(
        hand_out,
        out_shape=shapes,
        in_specs=[vm] * 5,
        out_specs=(any_space,) * 5,
        scratch_shapes=[pltpu.SemaphoreType.DMA((5,))],
        compiler_params=pltpu.CompilerParams(vmem_limit_bytes=VMEM_LIMIT),
        name="hand_out",
    )(*results)
    return out, grad_input, grad_qkv, grad_proj, grad_gain.reshape(width)


def solution(mesh):
    return jax.shard_map(
        functools.partial(body, mesh.shape["pts"], mesh.shape["tp"]),
        mesh=mesh,
        in_specs=(
            P("pts", None),
            P("pts", None),
            P("pts", None),
            P(),
            P(None, None, "tp"),
            P("tp", None),
            P("pts", None),
        ),
        out_specs=(P("pts", None), P("pts", None), P(None, None, "tp"), P("tp", None), P()),
        check_vma=False,
    )
```

```python
import functools

import jax
import jax.numpy as jnp
from jax import lax
from jax.experimental import pallas as pl
from jax.experimental.pallas import tpu as pltpu
from jax.sharding import PartitionSpec as P

MESH = pl.DeviceIdType.MESH
F32 = jnp.float32
BF16 = jnp.bfloat16
BLK = 128
NBLK = 8
KB = 4
LANES = 128
HALF = 64
EMPTY = 2e38
EMPTY_CUT = 1e38
LOW = -1e30
VMEM_LIMIT = 60 * 1024 * 1024
YS, ZS, CORES = 4, 4, 2


def ring(step, size):
    return min(step, size - step)


OFFSETS = sorted(
    [(y, z, c) for y in range(YS) for z in range(ZS) for c in range(CORES)][1:],
    key=lambda o: (-ring(o[0], YS) - ring(o[1], ZS), o),
)

CHIPS = [(y, z) for y, z, c in OFFSETS if c == 0]

(K_Q, K_V, K_G, K_CTX, K_BACK, K_UPD, K_OUT, K_N, K_IN, K_W, K_WALL, K_GAIN, K_GAINX, K_WO, K_WQKV) = (
    0, 1, 2, 3, 4, 7, 8, 9, 12, 13, 14, 15, 16, 17, 18
)
K_PAIR, K_FORWARD, PHASES = 19, 23, 24


def nn(a, b):
    return jnp.dot(a, b, preferred_element_type=F32)


def nt(a, b):
    return lax.dot_general(a, b, (((1,), (1,)), ((), ())), preferred_element_type=F32)


def wait_bytes(ref, sem):
    pltpu.make_async_copy(ref, ref, sem).wait()


def kernel(
    n,
    tp,
    pts_hbm,
    dest_hbm,
    pat_hbm,
    gain_hbm,
    wqkv_hbm,
    wo_hbm,
    gout_hbm,
    out_hbm,
    gin_hbm,
    gw_hbm,
    ggain_hbm,
    pts_ref,
    dest_ref,
    pat_ref,
    gain_ref,
    wqkv_all,
    wo_all,
    gout_ref,
    in_sem,
    out_sem,
    xhat,
    inv_std,
    normed,
    normed_t,
    gout_t,
    pick,
    put_all,
    rows_kq,
    rows_vg,
    kq_send,
    kq_recv,
    v_send,
    v_recv,
    g_send,
    g_recv,
    qs,
    gs,
    k_t,
    v_t,
    bias,
    probs,
    gk_part,
    gv_part,
    stack,
    ra_send,
    ra_recv,
    rb_send,
    rb_recv,
    c_send,
    c_recv,
    n_send,
    n_recv,
    acc,
    acc_gain,
    o_all,
    i_all,
    pair_send,
    pair_recv,
    gw_send,
    gw_recv,
    gw_all,
    gg_recv,
    gx_recv,
    gain_out,
    ssem,
    rsem,
):
    me = lax.axis_index("pts")
    tm = lax.axis_index("tp")
    cap = kq_send.shape[1]
    per_blk = BLK // cap
    points, width = pts_ref.shape
    slots = n * cap
    chunk = points // tp
    my_y = me // (ZS * CORES)
    my_z = lax.rem(me // CORES, ZS)
    my_c = lax.rem(me, CORES)

    barrier = pltpu.get_barrier_semaphore()

    def greet(i, carry):
        pl.semaphore_signal(
            barrier, inc=1, device_id=(lax.rem(me + i, n), tm), device_id_type=MESH
        )
        return carry

    for i in range(1, tp):
        pl.semaphore_signal(
            barrier, inc=1, device_id=(me, lax.rem(tm + i, tp)), device_id_type=MESH
        )
    lax.fori_loop(1, n, greet, 0)

    fetches = [
        pltpu.make_async_copy(src, dst, in_sem.at[i])
        for i, (src, dst) in enumerate(
            (
                (dest_hbm, dest_ref),
                (pts_hbm, pts_ref),
                (gain_hbm, gain_ref),
                (wqkv_hbm, wqkv_all.at[tm]),
                (gout_hbm, gout_ref),
                (wo_hbm, wo_all.at[tm]),
                (pat_hbm, pat_ref),
            )
        )
    ]
    for fetch in fetches:
        fetch.start()

    def remote(src, dst, phase, peer):
        return pltpu.make_async_remote_copy(
            src_ref=src,
            dst_ref=dst,
            send_sem=ssem.at[phase],
            recv_sem=rsem.at[phase],
            device_id=peer,
            device_id_type=MESH,
        )

    def to_pts(send, recv, phase):
        for dy, dz, dc in OFFSETS:
            peer = (lax.rem(my_y + dy, YS) * ZS + lax.rem(my_z + dz, ZS)) * CORES
            peer = peer + lax.rem(my_c + dc, CORES)
            remote(send(peer), recv.at[me], phase, (peer, tm)).start()

    chips = n // CORES
    my_chip = me // CORES
    twin = (me + 1 - 2 * my_c, tm)

    def to_chips(send, recv, phase):
        for dy, dz in CHIPS:
            chip = lax.rem(my_y + dy, YS) * ZS + lax.rem(my_z + dz, ZS)
            remote(send(chip), recv.at[my_chip], phase, (chip * CORES + my_c, tm)).start()

    def pair(which, rows):
        pair_send[which] = rows.reshape(pair_send.shape[1:])
        remote(
            pair_send.at[which, 1 - my_c], pair_recv.at[which], K_PAIR + which, twin
        ).start()

    def fold(which):
        wait_bytes(pair_recv.at[which], rsem.at[K_PAIR + which])
        both = pair_send[which, my_c].astype(F32) + pair_recv[which].astype(F32)
        gw_send[:, which] = both.astype(BF16).reshape(chips, width // n, LANES)

    def to_tp(send, recv, phase):
        for i in range(1, tp):
            peer = lax.rem(tm + i, tp)
            remote(send(peer), recv(tm), phase, (me, peer)).start()

    def nth(i):
        dy = jnp.where(i < 2, 2, jnp.where(i < 6, 1 + 2 * lax.rem(i, 2), 0))
        dz = jnp.where(i < 2, 1 - i, jnp.where(i < 6, 1 - (i - 2) // 2, 7 - i))
        return lax.rem(my_y + dy, YS) * 2 + lax.rem(my_z // 2 + dz, 2)

    def blocks(step, work, order=None):
        def some(i, carry):
            at = [i * step + k for k in range(step)]
            work([order(a) for a in at] if order else at)
            return carry

        lax.fori_loop(0, NBLK // step, some, 0)

    def to_group(send, recv, phase, b, which):
        for u in which:
            peer = b * per_blk + u

            @pl.when(peer != me)
            def _():
                remote(send.at[peer], recv.at[me], phase, (peer, tm)).start()

    upto = jnp.where(
        lax.broadcasted_iota(jnp.int32, (points, points), 0)
        <= lax.broadcasted_iota(jnp.int32, (points, points), 1),
        1.0,
        0.0,
    ).astype(BF16)
    fetches[0].wait()
    dest = dest_ref[...].astype(F32)
    owner = lax.broadcasted_iota(jnp.int32, (n, points), 0).astype(F32)
    onehot = jnp.where(dest == owner, 1.0, 0.0)
    count = nn(onehot.astype(BF16), upto)
    index = dest * cap + jnp.sum(count * onehot, 0, keepdims=True) - 1.0

    fetches[1].wait()
    fetches[2].wait()

    def norm(r, carry):
        at = pl.ds(pl.multiple_of(r * BLK, BLK), BLK)
        x = pts_ref[at, :].astype(F32)
        shifted = x - jnp.mean(x, -1, keepdims=True)
        inv = lax.rsqrt(jnp.mean(shifted * shifted, -1, keepdims=True) + 1e-05)
        hat = shifted * inv
        xhat[at, :] = hat
        inv_std[at, :] = inv
        normed[at, :] = (hat * gain_ref[...]).astype(BF16)
        return carry

    lax.fori_loop(0, points // BLK, norm, 0)
    fetches[3].wait()
    nm = normed[...]
    rows_kq[:, 0:LANES] = nn(nm, wqkv_all[tm, 1]).astype(BF16)
    rows_kq[:, LANES : 2 * LANES] = (nn(nm, wqkv_all[tm, 0]).astype(BF16).astype(F32) * 0.125).astype(
        BF16
    )
    slot_sub = lax.broadcasted_iota(jnp.int32, (BLK, points), 0).astype(F32)
    ones = jnp.ones((points, LANES), BF16)

    pl.semaphore_wait(barrier, n - 1 + tp - 1)

    def place(some):
        puts = [
            jnp.where(slot_sub + (c * BLK).astype(F32) == index, 1.0, 0.0).astype(BF16)
            for c in some
        ]
        lives = [nn(put, ones) for put in puts]
        kqs = [nn(put, rows_kq[...]) for put in puts]
        for c, put, live, kq in zip(some, puts, lives, kqs):
            put_all[c] = put
            k = kq[:, 0:LANES].astype(BF16)
            q = jnp.where(live > 0.5, kq[:, LANES : 2 * LANES], EMPTY).astype(BF16)
            at = pl.ds(c * per_blk, per_blk)
            kq_send[at, :, 0:LANES] = k.reshape(per_blk, cap, LANES)
            kq_send[at, :, LANES : 2 * LANES] = q.reshape(per_blk, cap, LANES)
        for c in some:
            to_group(kq_send, kq_recv, K_Q, c, range(per_blk))

    blocks(2, place, nth)
    kq_recv[me] = kq_send[me]

    fetches[4].wait()
    fetches[5].wait()
    to_tp(lambda peer: wo_all.at[tm], lambda at: wo_all.at[at], K_WO)
    to_tp(lambda peer: wqkv_all.at[tm], lambda at: wqkv_all.at[at], K_WQKV)
    rows_vg[:, 0:LANES] = nn(nm, wqkv_all[tm, 2]).astype(BF16)
    rows_vg[:, LANES : 2 * LANES] = nt(gout_ref[...], wo_all[tm]).astype(BF16)

    def place_more(some):
        vgs = [nn(put_all[c], rows_vg[...]).astype(BF16) for c in some]
        for c, vg in zip(some, vgs):
            at = pl.ds(c * per_blk, per_blk)
            v_send[at] = vg[:, 0:LANES].reshape(per_blk, cap, LANES)
            g_send[at] = vg[:, LANES : 2 * LANES].reshape(per_blk, cap, LANES)
        for c in some:
            to_group(v_send, v_recv, K_V, c, range(per_blk))

    blocks(4, place_more, nth)
    to_pts(lambda peer: g_send.at[peer], g_recv, K_G)
    v_recv[me] = v_send[me]
    g_recv[me] = g_send[me]

    fetches[6].wait()
    index_col = jnp.broadcast_to(index, (LANES, points)).T
    lane = lax.broadcasted_iota(jnp.int32, (points, LANES), 1).astype(F32)
    for t in range(slots // LANES):
        pick[:, t * LANES : (t + 1) * LANES] = jnp.where(
            index_col == lane + t * LANES, 1.0, 0.0
        ).astype(BF16)
    normed_t[...] = nm.astype(F32).T.astype(BF16)
    gout_t[...] = gout_ref[...].astype(F32).T.astype(BF16)
    gk_part[:, KB] = jnp.zeros((NBLK, BLK, LANES), F32)
    gv_part[:, KB] = jnp.zeros((NBLK, BLK, LANES), F32)

    head_lane = lax.broadcasted_iota(jnp.int32, (BLK, LANES), 1) < HALF
    head_sub = lax.broadcasted_iota(jnp.int32, (LANES, BLK), 0) < HALF

    def block_of(ref, b, first=0):
        return ref[pl.ds(b * per_blk, per_blk), :, first : first + LANES].reshape(BLK, LANES)

    def halves(ref, b, rows):
        ref[b, 0:BLK] = jnp.where(head_lane, rows, 0.0).astype(BF16)
        ref[b, BLK : 2 * BLK] = jnp.where(head_lane, 0.0, rows).astype(BF16)

    def chosen_of(b):
        return [pat_ref[j, b] for j in range(KB)]

    wait_bytes(kq_recv.at[pl.ds(0, n - 1)], rsem.at[K_Q])

    def prepare(some):
        for b in some:
            q = block_of(kq_recv, b, LANES).astype(F32)
            empty = q > EMPTY_CUT
            bias[b] = jnp.where(empty, LOW, 0.0)
            halves(qs, b, jnp.where(empty, 0.0, q))
            k_t[b] = block_of(kq_recv, b).astype(F32).T.astype(BF16)

    blocks(8, prepare)

    def softmax(some):
        scores = []
        for b in some:
            chosen = chosen_of(b)
            keys = jnp.concatenate([block_of(kq_recv, c) for c in chosen], 0)
            low = jnp.concatenate([bias[c] for c in chosen], 0)
            scores.append(nt(keys, qs[b]) + jnp.concatenate([low, low], 1))
        for b, score in zip(some, scores):
            raised = jnp.exp(score - jnp.max(score, 0, keepdims=True))
            p = raised * (1.0 / jnp.sum(raised, 0, keepdims=True))
            probs[b] = p.astype(BF16)

    blocks(8, softmax)

    wait_bytes(v_recv.at[pl.ds(0, n - 1)], rsem.at[K_V])

    def prepare_v(some):
        for b in some:
            v_t[b] = block_of(v_recv, b).astype(F32).T.astype(BF16)

    blocks(8, prepare_v)

    def mix(some):
        ctx_t = [
            nn(jnp.concatenate([v_t[c] for c in chosen_of(b)], 1), probs[b]) for b in some
        ]
        ctx = [jnp.where(head_sub, c[:, 0:BLK], c[:, BLK : 2 * BLK]).T.astype(BF16) for c in ctx_t]
        for b, c in zip(some, ctx):
            ra_send[pl.ds(b * per_blk, per_blk)] = c.reshape(per_blk, cap, LANES)
        for b in some:
            to_group(ra_send, ra_recv, K_CTX, b, range(per_blk))

    blocks(8, mix, nth)
    ra_recv[me] = ra_send[me]

    wait_bytes(g_recv.at[pl.ds(0, n - 1)], rsem.at[K_G])

    def prepare_g(some):
        for b in some:
            halves(gs, b, block_of(g_recv, b).astype(F32))

    blocks(8, prepare_g)

    def interleave(b, first, count):
        for j in range(3):
            some = stack[b, pl.ds(3 * cap * first + j, cap * count, stride=3), :]
            rb_send[j, pl.ds(b * per_blk + first, count)] = some.astype(BF16).reshape(
                count, cap, LANES
            )

    def grads_of(some):
        dps = [
            nt(jnp.concatenate([block_of(v_recv, c) for c in chosen_of(b)], 0), gs[b])
            for b in some
        ]
        dss = []
        for b, dp in zip(some, dps):
            gv_part[b, 0:KB] = nn(probs[b], gs[b]).reshape(KB, BLK, LANES)
            p = probs[b].astype(F32)
            delta = jnp.sum(p * dp, 0, keepdims=True)
            dss.append((p * (dp - delta)).astype(BF16))
        gqs = []
        for b, ds in zip(some, dss):
            gq_t = nn(jnp.concatenate([k_t[c] for c in chosen_of(b)], 1), ds)
            gk_part[b, 0:KB] = nn(ds, qs[b]).reshape(KB, BLK, LANES)
            gqs.append(jnp.where(head_sub, gq_t[:, 0:BLK], gq_t[:, BLK : 2 * BLK]).T * 0.125)
        for b, gq in zip(some, gqs):
            stack[b, 0:BLK] = gq
        for b in some:
            interleave(b, 0, 1)
        for b in some:
            for j in range(3):
                to_group(rb_send.at[j], rb_recv.at[j], K_BACK + j, b, range(1))

    blocks(8, grads_of, nth)

    def key_side(some):
        for c in some:
            gk = jnp.zeros((BLK, LANES), F32)
            gv = jnp.zeros((BLK, LANES), F32)
            for b in range(NBLK):
                j = jnp.int32(KB)
                for which in range(KB):
                    j = jnp.where(pat_ref[which, b] == c, which, j)
                gk = gk + gk_part[b, j]
                gv = gv + gv_part[b, j]
            stack[c, BLK : 2 * BLK] = gk
            stack[c, 2 * BLK : 3 * BLK] = gv
        for c in some:
            interleave(c, 1, per_blk - 1)
        for c in some:
            to_group(rb_send.at[0], rb_recv.at[0], K_BACK, c, range(1, per_blk))

    blocks(8, key_side, nth)

    def send_slab(j):
        def one(i, carry):
            to_group(rb_send.at[j], rb_recv.at[j], K_BACK + j, nth(i), range(1, per_blk))
            return carry

        lax.fori_loop(0, NBLK, one, 0)

    send_slab(1)
    send_slab(2)
    for j in range(3):
        rb_recv[j, me] = rb_send[j, me]

    wait_bytes(ra_recv.at[pl.ds(0, n - 1)], rsem.at[K_CTX])
    context = nn(pick[...], ra_recv[...].reshape(slots, LANES)).astype(BF16)
    c_send[...] = context.reshape(tp, chunk, LANES)
    to_tp(lambda peer: c_send.at[peer], lambda at: c_recv.at[at], K_UPD)

    pair(3, nn(gout_t[...], c_send[...].reshape(points, LANES)).astype(BF16))
    c_recv[tm] = c_send[tm]
    wait_bytes(wo_all.at[pl.ds(0, tp - 1)], rsem.at[K_WO])
    wait_bytes(c_recv.at[pl.ds(0, tp - 1)], rsem.at[K_UPD])
    mine = pl.ds(pl.multiple_of(tm * chunk, chunk), chunk)
    update = sum(nn(c_recv[t], wo_all[t]) for t in range(tp)).astype(BF16).astype(F32)
    o_all[tm] = (pts_ref[mine, :].astype(F32) + update).astype(BF16)
    to_tp(lambda peer: o_all.at[tm], lambda at: o_all.at[at], K_OUT)
    wait_bytes(wqkv_all.at[pl.ds(0, tp - 1)], rsem.at[K_WQKV])

    acc[...] = jnp.zeros_like(acc)

    def add_rows(j):
        n_recv[j, tm] = n_send[j, tm]
        wait_bytes(n_recv.at[j, pl.ds(0, tp - 1)], rsem.at[K_N + j])
        acc[...] += sum(nt(n_recv[j, t], wqkv_all[t, j]) for t in range(tp))

    for j in range(3):
        wait_bytes(rb_recv.at[j, pl.ds(0, n - 1)], rsem.at[K_BACK + j])
        rows = nn(pick[...], rb_recv[j].reshape(slots, LANES)).astype(BF16)
        n_send[j] = rows.reshape(tp, chunk, LANES)
        to_tp(lambda peer: n_send.at[j, peer], lambda at: n_recv.at[j, at], K_N + j)
        gw = nn(normed_t[...], rows)
        pair(j, gw.astype(BF16))
        weighted = gw * wqkv_all[tm, j].astype(F32)
        acc_gain[...] = weighted if j == 0 else acc_gain[...] + weighted
    gain_part = jnp.sum(acc_gain[...].T, 0, keepdims=True) / gain_ref[...]
    for j in range(width // LANES):
        gg_recv[me, j] = gain_part[:, j * LANES : (j + 1) * LANES]
    to_pts(lambda peer: gg_recv.at[me], gg_recv, K_GAIN)
    for which in (3, 0, 1, 2):
        fold(which)
    to_chips(lambda chip: gw_send.at[chip], gw_recv, K_W)

    add_rows(0)
    add_rows(1)
    wait_bytes(gg_recv.at[pl.ds(0, n - 1)], rsem.at[K_GAIN])
    gx_recv[tm] = jnp.sum(gg_recv[...], 0)
    to_tp(lambda peer: gx_recv.at[tm], lambda at: gx_recv.at[at], K_GAINX)
    add_rows(2)
    grad = acc[...]
    grad = grad.astype(BF16).astype(F32)
    hat = xhat[mine, :]
    scaled = grad * gain_ref[...]
    first = jnp.mean(scaled, -1, keepdims=True)
    second = jnp.mean(scaled * hat, -1, keepdims=True)
    branch = (inv_std[mine, :] * (scaled - first - hat * second)).astype(BF16).astype(F32)
    i_all[tm] = (gout_ref[mine, :].astype(F32) + branch).astype(BF16)
    to_tp(lambda peer: i_all.at[tm], lambda at: i_all.at[at], K_IN)

    gw_recv[my_chip] = gw_send[my_chip]
    wait_bytes(gw_recv.at[pl.ds(0, chips - 1)], rsem.at[K_W])
    gw_all[my_c, my_chip] = jnp.sum(gw_recv[...].astype(F32), 0).astype(BF16)
    to_chips(lambda chip: gw_all.at[my_c, my_chip], gw_all.at[my_c], K_WALL)

    def hand(src, dst, which):
        copy = pltpu.make_async_copy(src, dst, out_sem.at[which])
        copy.start()
        return copy

    wait_bytes(o_all.at[pl.ds(0, tp - 1)], rsem.at[K_OUT])
    handed = [hand(o_all, out_hbm, 0)]

    for phase, buf in (
        (K_Q, kq_send),
        (K_V, v_send),
        (K_G, g_send),
        (K_CTX, ra_send),
        (K_BACK, rb_send.at[0]),
        (K_BACK + 1, rb_send.at[1]),
        (K_BACK + 2, rb_send.at[2]),
        (K_GAIN, gg_recv),
    ):
        wait_bytes(buf.at[pl.ds(0, n - 1)], ssem.at[phase])
    for phase, buf in (
        (K_WO, wo_all),
        (K_WQKV, wqkv_all),
        (K_UPD, c_send),
        (K_OUT, o_all),
        (K_N, n_send.at[0]),
        (K_N + 1, n_send.at[1]),
        (K_N + 2, n_send.at[2]),
    ):
        wait_bytes(buf.at[pl.ds(0, tp - 1)], ssem.at[phase])

    wait_bytes(gw_all.at[my_c, pl.ds(0, chips - 1)], rsem.at[K_WALL])
    remote(gw_all.at[my_c], gw_all.at[my_c], K_FORWARD, twin).start()
    wait_bytes(gx_recv.at[pl.ds(0, tp - 1)], rsem.at[K_GAINX])
    gain_sum = jnp.sum(gx_recv[...], 0)
    for j in range(width // LANES):
        gain_out[:, j * LANES : (j + 1) * LANES] = gain_sum[j]
    handed.append(hand(gain_out, ggain_hbm, 1))
    wait_bytes(i_all.at[pl.ds(0, tp - 1)], rsem.at[K_IN])
    handed.append(hand(i_all, gin_hbm, 2))
    wait_bytes(gw_all.at[1 - my_c], rsem.at[K_FORWARD])
    handed.append(hand(gw_all, gw_hbm, 3))
    for phase, buf in ((K_IN, i_all), (K_GAINX, gx_recv)):
        wait_bytes(buf.at[pl.ds(0, tp - 1)], ssem.at[phase])
    wait_bytes(gw_send.at[pl.ds(0, chips - 1)], ssem.at[K_W])
    wait_bytes(gw_all.at[my_c, pl.ds(0, chips - 1)], ssem.at[K_WALL])
    wait_bytes(gw_all.at[my_c], ssem.at[K_FORWARD])
    for which in range(4):
        wait_bytes(pair_recv.at[which], ssem.at[K_PAIR + which])
    for copy in handed:
        copy.wait()


def hand_out(
    out_in,
    gin_in,
    gw_in,
    gain_in,
    out_ref,
    gin_ref,
    gqkv_ref,
    gproj_ref,
    gain_ref,
    out_buf,
    gin_buf,
    gw_buf,
    gain_buf,
    gqkv_buf,
    gproj_buf,
    sems,
):
    def copy(src, dst, which):
        one = pltpu.make_async_copy(src, dst, sems.at[which])
        one.start()
        return one

    gw_get = copy(gw_in, gw_buf, 0)
    out_get = copy(out_in, out_buf, 1)
    gin_get = copy(gin_in, gin_buf, 2)
    gain_get = copy(gain_in, gain_buf, 3)
    width = out_buf.shape[1]

    def whole(which):
        return gw_buf[:, :, which].reshape(width, LANES).astype(F32)

    puts = []
    gw_get.wait()
    for j in range(3):
        gqkv_buf[j] = whole(j)
    puts.append(copy(gqkv_buf, gqkv_ref, 4))
    out_get.wait()
    puts.append(copy(out_buf, out_ref, 5))
    gin_get.wait()
    puts.append(copy(gin_buf, gin_ref, 6))
    gproj_buf[...] = whole(3).T
    puts.append(copy(gproj_buf, gproj_ref, 7))
    gain_get.wait()
    puts.append(copy(gain_buf, gain_ref, 8))
    for put in puts:
        put.wait()


def body(n, tp, points, destination, pattern, norm_gain, qkv_weight, out_weight, grad_out):
    rows, width = points.shape
    cap = 2 * rows // n
    slots = n * cap
    chunk = rows // tp
    hbm = pl.BlockSpec(memory_space=pltpu.HBM)
    scratch = [
        pltpu.VMEM((rows, width), BF16),
        pltpu.VMEM((1, rows), jnp.int32),
        pltpu.SMEM((KB, NBLK), jnp.int32),
        pltpu.VMEM((1, width), F32),
        pltpu.VMEM((tp, 3, width, LANES), BF16),
        pltpu.VMEM((tp, LANES, width), BF16),
        pltpu.VMEM((rows, width), BF16),
        pltpu.SemaphoreType.DMA((7,)),
        pltpu.SemaphoreType.DMA((4,)),
        pltpu.VMEM((rows, width), F32),
        pltpu.VMEM((rows, 1), F32),
        pltpu.VMEM((rows, width), BF16),
        pltpu.VMEM((width, rows), BF16),
        pltpu.VMEM((width, rows), BF16),
        pltpu.VMEM((rows, slots), BF16),
        pltpu.VMEM((NBLK, BLK, rows), BF16),
        pltpu.VMEM((rows, 2 * LANES), BF16),
        pltpu.VMEM((rows, 2 * LANES), BF16),
        pltpu.VMEM((n, cap, 2 * LANES), BF16),
        pltpu.VMEM((n, cap, 2 * LANES), BF16),
        pltpu.VMEM((n, cap, LANES), BF16),
        pltpu.VMEM((n, cap, LANES), BF16),
        pltpu.VMEM((n, cap, LANES), BF16),
        pltpu.VMEM((n, cap, LANES), BF16),
        pltpu.VMEM((NBLK, 2 * BLK, LANES), BF16),
        pltpu.VMEM((NBLK, 2 * BLK, LANES), BF16),
        pltpu.VMEM((NBLK, LANES, BLK), BF16),
        pltpu.VMEM((NBLK, LANES, BLK), BF16),
        pltpu.VMEM((NBLK, BLK, LANES), F32),
        pltpu.VMEM((NBLK, KB * BLK, 2 * BLK), BF16),
        pltpu.VMEM((NBLK, KB + 1, BLK, LANES), F32),
        pltpu.VMEM((NBLK, KB + 1, BLK, LANES), F32),
        pltpu.VMEM((NBLK, 3 * BLK, LANES), F32),
        pltpu.VMEM((n, cap, LANES), BF16),
        pltpu.VMEM((n, cap, LANES), BF16),
        pltpu.VMEM((3, n, cap, LANES), BF16),
        pltpu.VMEM((3, n, cap, LANES), BF16),
        pltpu.VMEM((tp, chunk, LANES), BF16),
        pltpu.VMEM((tp, chunk, LANES), BF16),
        pltpu.VMEM((3, tp, chunk, LANES), BF16),
        pltpu.VMEM((3, tp, chunk, LANES), BF16),
        pltpu.VMEM((chunk, width), F32),
        pltpu.VMEM((width, LANES), F32),
        pltpu.VMEM((tp, chunk, width), BF16),
        pltpu.VMEM((tp, chunk, width), BF16),
        pltpu.VMEM((4, CORES, width // CORES, LANES), BF16),
        pltpu.VMEM((4, width // CORES, LANES), BF16),
        pltpu.VMEM((n // CORES, 4, width // n, LANES), BF16),
        pltpu.VMEM((n // CORES, 4, width // n, LANES), BF16),
        pltpu.VMEM((CORES, n // CORES, 4, width // n, LANES), BF16),
        pltpu.VMEM((n, width // LANES, 1, LANES), F32),
        pltpu.VMEM((tp, width // LANES, 1, LANES), F32),
        pltpu.VMEM((1, width), F32),
        pltpu.SemaphoreType.DMA((PHASES,)),
        pltpu.SemaphoreType.DMA((PHASES,)),
    ]
    out_shape = jax.ShapeDtypeStruct((rows, width), BF16)
    gain_shape = jax.ShapeDtypeStruct((1, width), F32)
    qkv_shape = jax.ShapeDtypeStruct((3, width, LANES), F32)
    proj_shape = jax.ShapeDtypeStruct((LANES, width), F32)
    by_tp = jax.ShapeDtypeStruct((tp, chunk, width), BF16)
    parts = jax.ShapeDtypeStruct((CORES, n // CORES, 4, width // n, LANES), BF16)
    out, grad_input, grads, gain = pl.pallas_call(
        functools.partial(kernel, n, tp),
        out_shape=(by_tp, by_tp, parts, gain_shape),
        in_specs=[hbm] * 7,
        out_specs=(hbm,) * 4,
        scratch_shapes=scratch,
        compiler_params=pltpu.CompilerParams(
            collective_id=0, has_side_effects=True, vmem_limit_bytes=VMEM_LIMIT
        ),
        name="point_attention",
    )(
        points,
        destination.reshape(1, rows),
        pattern.T,
        norm_gain.reshape(1, width),
        qkv_weight,
        out_weight,
        grad_out,
    )
    out, grad_input, grad_qkv, grad_proj, grad_gain = pl.pallas_call(
        hand_out,
        out_shape=(out_shape, out_shape, qkv_shape, proj_shape, gain_shape),
        in_specs=[hbm] * 4,
        out_specs=(hbm,) * 5,
        scratch_shapes=[
            pltpu.VMEM((rows, width), BF16),
            pltpu.VMEM((rows, width), BF16),
            pltpu.VMEM((CORES, n // CORES, 4, width // n, LANES), BF16),
            pltpu.VMEM((1, width), F32),
            pltpu.VMEM((3, width, LANES), F32),
            pltpu.VMEM((LANES, width), F32),
            pltpu.SemaphoreType.DMA((9,)),
        ],
        compiler_params=pltpu.CompilerParams(vmem_limit_bytes=VMEM_LIMIT),
        name="hand_out",
    )(out.reshape(rows, width), grad_input.reshape(rows, width), grads, gain)
    return out, grad_input, grad_qkv, grad_proj, grad_gain.reshape(width)


def solution(mesh):
    return jax.shard_map(
        functools.partial(body, mesh.shape["pts"], mesh.shape["tp"]),
        mesh=mesh,
        in_specs=(
            P("pts", None),
            P("pts", None),
            P("pts", None),
            P(),
            P(None, None, "tp"),
            P("tp", None),
            P("pts", None),
        ),
        out_specs=(P("pts", None), P("pts", None), P(None, None, "tp"), P("tp", None), P()),
        check_vma=False,
    )
```

```python
import functools

import jax
import jax.numpy as jnp
from jax import lax
from jax.experimental import pallas as pl
from jax.experimental.pallas import tpu as pltpu
from jax.sharding import PartitionSpec as P

MESH = pl.DeviceIdType.MESH
F32 = jnp.float32
BF16 = jnp.bfloat16
BLK = 128
NBLK = 8
KB = 4
LANES = 128
HALF = 64
EMPTY = 2e38
EMPTY_CUT = 1e38
LOW = -1e30
VMEM_LIMIT = 60 * 1024 * 1024
YS, ZS, CORES = 4, 4, 2


def ring(step, size):
    return min(step, size - step)


OFFSETS = sorted(
    [(y, z, c) for y in range(YS) for z in range(ZS) for c in range(CORES)][1:],
    key=lambda o: (-ring(o[0], YS) - ring(o[1], ZS), o),
)

CHIPS = [(y, z) for y, z, c in OFFSETS if c == 0]

(K_Q, K_V, K_G, K_CTX, K_BACK, K_UPD, K_OUT, K_N, K_IN, K_W, K_WALL, K_GAIN, K_GAINX, K_WO, K_WQKV) = (
    0, 1, 2, 3, 4, 7, 8, 9, 12, 13, 14, 15, 16, 17, 18
)
K_PAIR, K_FORWARD, K_OUT_REST, K_GAIN_PAIR, PHASES = 19, 23, 24, 25, 26


def nn(a, b):
    return jnp.dot(a, b, preferred_element_type=F32)


def nt(a, b):
    return lax.dot_general(a, b, (((1,), (1,)), ((), ())), preferred_element_type=F32)


def wait_bytes(ref, sem):
    pltpu.make_async_copy(ref, ref, sem).wait()


def kernel(
    n,
    tp,
    pts_hbm,
    dest_hbm,
    pat_hbm,
    gain_hbm,
    wqkv_hbm,
    wo_hbm,
    gout_hbm,
    out_hbm,
    gin_hbm,
    gw_hbm,
    ggain_hbm,
    pts_ref,
    dest_ref,
    pat_ref,
    gain_ref,
    wqkv_all,
    wo_all,
    gout_ref,
    in_sem,
    out_sem,
    xhat,
    inv_std,
    normed,
    normed_t,
    gout_t,
    pick,
    put_all,
    rows_kq,
    rows_vg,
    kq_send,
    kq_recv,
    v_send,
    v_recv,
    g_send,
    g_recv,
    qs,
    gs,
    k_t,
    v_t,
    bias,
    probs,
    gk_part,
    gv_part,
    stack,
    ra_send,
    ra_recv,
    rb_send,
    rb_recv,
    c_send,
    c_recv,
    n_send,
    n_recv,
    acc,
    acc_gain,
    o_all,
    i_all,
    pair_send,
    pair_recv,
    gw_send,
    gw_recv,
    gw_all,
    gg_own,
    gg_twin,
    gg_recv,
    gx_recv,
    gain_out,
    ssem,
    rsem,
):
    me = lax.axis_index("pts")
    tm = lax.axis_index("tp")
    cap = kq_send.shape[1]
    per_blk = BLK // cap
    points, width = pts_ref.shape
    slots = n * cap
    chunk = points // tp
    my_y = me // (ZS * CORES)
    my_z = lax.rem(me // CORES, ZS)
    my_c = lax.rem(me, CORES)

    barrier = pltpu.get_barrier_semaphore()

    def greet(i, carry):
        pl.semaphore_signal(
            barrier, inc=1, device_id=(lax.rem(me + i, n), tm), device_id_type=MESH
        )
        return carry

    for i in range(1, tp):
        pl.semaphore_signal(
            barrier, inc=1, device_id=(me, lax.rem(tm + i, tp)), device_id_type=MESH
        )
    lax.fori_loop(1, n, greet, 0)

    fetches = [
        pltpu.make_async_copy(src, dst, in_sem.at[i])
        for i, (src, dst) in enumerate(
            (
                (dest_hbm, dest_ref),
                (pts_hbm, pts_ref),
                (gain_hbm, gain_ref),
                (wqkv_hbm, wqkv_all.at[tm]),
                (gout_hbm, gout_ref),
                (wo_hbm, wo_all.at[tm]),
                (pat_hbm, pat_ref),
            )
        )
    ]
    for fetch in fetches:
        fetch.start()

    def remote(src, dst, phase, peer):
        return pltpu.make_async_remote_copy(
            src_ref=src,
            dst_ref=dst,
            send_sem=ssem.at[phase],
            recv_sem=rsem.at[phase],
            device_id=peer,
            device_id_type=MESH,
        )

    def to_pts(send, recv, phase):
        for dy, dz, dc in OFFSETS:
            peer = (lax.rem(my_y + dy, YS) * ZS + lax.rem(my_z + dz, ZS)) * CORES
            peer = peer + lax.rem(my_c + dc, CORES)
            remote(send(peer), recv.at[me], phase, (peer, tm)).start()

    chips = n // CORES
    my_chip = me // CORES
    twin = (me + 1 - 2 * my_c, tm)

    def to_chips(send, recv, phase):
        for dy, dz in CHIPS:
            chip = lax.rem(my_y + dy, YS) * ZS + lax.rem(my_z + dz, ZS)
            remote(send(chip), recv.at[my_chip], phase, (chip * CORES + my_c, tm)).start()

    def pair(which, rows):
        pair_send[which] = rows.reshape(pair_send.shape[1:])
        remote(
            pair_send.at[which, 1 - my_c], pair_recv.at[which], K_PAIR + which, twin
        ).start()

    def fold(which):
        wait_bytes(pair_recv.at[which], rsem.at[K_PAIR + which])
        both = pair_send[which, my_c].astype(F32) + pair_recv[which].astype(F32)
        gw_send[:, which] = both.astype(BF16).reshape(chips, width // n, LANES)

    def to_tp(send, recv, phase):
        for i in range(1, tp):
            peer = lax.rem(tm + i, tp)
            remote(send(peer), recv(tm), phase, (me, peer)).start()

    def nth(i):
        dy = jnp.where(i < 2, 2, jnp.where(i < 6, 1 + 2 * lax.rem(i, 2), 0))
        dz = jnp.where(i < 2, 1 - i, jnp.where(i < 6, 1 - (i - 2) // 2, 7 - i))
        return lax.rem(my_y + dy, YS) * 2 + lax.rem(my_z // 2 + dz, 2)

    def blocks(step, work, order=None):
        def some(i, carry):
            at = [i * step + k for k in range(step)]
            work([order(a) for a in at] if order else at)
            return carry

        lax.fori_loop(0, NBLK // step, some, 0)

    def to_group(send, recv, phase, b, which):
        for u in which:
            peer = b * per_blk + u

            @pl.when(peer != me)
            def _():
                remote(send.at[peer], recv.at[me], phase, (peer, tm)).start()

    upto = jnp.where(
        lax.broadcasted_iota(jnp.int32, (points, points), 0)
        <= lax.broadcasted_iota(jnp.int32, (points, points), 1),
        1.0,
        0.0,
    ).astype(BF16)
    fetches[0].wait()
    dest = dest_ref[...].astype(F32)
    owner = lax.broadcasted_iota(jnp.int32, (n, points), 0).astype(F32)
    onehot = jnp.where(dest == owner, 1.0, 0.0)
    count = nn(onehot.astype(BF16), upto)
    index = dest * cap + jnp.sum(count * onehot, 0, keepdims=True) - 1.0

    fetches[1].wait()
    fetches[2].wait()

    def norm(r, carry):
        at = pl.ds(pl.multiple_of(r * BLK, BLK), BLK)
        x = pts_ref[at, :].astype(F32)
        shifted = x - jnp.mean(x, -1, keepdims=True)
        inv = lax.rsqrt(jnp.mean(shifted * shifted, -1, keepdims=True) + 1e-05)
        hat = shifted * inv
        xhat[at, :] = hat
        inv_std[at, :] = inv
        normed[at, :] = (hat * gain_ref[...]).astype(BF16)
        return carry

    lax.fori_loop(0, points // BLK, norm, 0)
    fetches[3].wait()
    nm = normed[...]
    rows_kq[:, 0:LANES] = nn(nm, wqkv_all[tm, 1]).astype(BF16)
    rows_kq[:, LANES : 2 * LANES] = (nn(nm, wqkv_all[tm, 0]).astype(BF16).astype(F32) * 0.125).astype(
        BF16
    )
    slot_sub = lax.broadcasted_iota(jnp.int32, (BLK, points), 0).astype(F32)
    ones = jnp.ones((points, LANES), BF16)

    pl.semaphore_wait(barrier, n - 1 + tp - 1)

    def place(some):
        puts = [
            jnp.where(slot_sub + (c * BLK).astype(F32) == index, 1.0, 0.0).astype(BF16)
            for c in some
        ]
        lives = [nn(put, ones) for put in puts]
        kqs = [nn(put, rows_kq[...]) for put in puts]
        for c, put, live, kq in zip(some, puts, lives, kqs):
            put_all[c] = put
            k = kq[:, 0:LANES].astype(BF16)
            q = jnp.where(live > 0.5, kq[:, LANES : 2 * LANES], EMPTY).astype(BF16)
            at = pl.ds(c * per_blk, per_blk)
            kq_send[at, :, 0:LANES] = k.reshape(per_blk, cap, LANES)
            kq_send[at, :, LANES : 2 * LANES] = q.reshape(per_blk, cap, LANES)
        for c in some:
            to_group(kq_send, kq_recv, K_Q, c, range(per_blk))

    blocks(2, place, nth)
    kq_recv[me] = kq_send[me]

    fetches[4].wait()
    fetches[5].wait()
    to_tp(lambda peer: wo_all.at[tm], lambda at: wo_all.at[at], K_WO)
    to_tp(lambda peer: wqkv_all.at[tm], lambda at: wqkv_all.at[at], K_WQKV)
    rows_vg[:, 0:LANES] = nn(nm, wqkv_all[tm, 2]).astype(BF16)
    rows_vg[:, LANES : 2 * LANES] = nt(gout_ref[...], wo_all[tm]).astype(BF16)

    def place_more(some):
        vgs = [nn(put_all[c], rows_vg[...]).astype(BF16) for c in some]
        for c, vg in zip(some, vgs):
            at = pl.ds(c * per_blk, per_blk)
            v_send[at] = vg[:, 0:LANES].reshape(per_blk, cap, LANES)
            g_send[at] = vg[:, LANES : 2 * LANES].reshape(per_blk, cap, LANES)
        for c in some:
            to_group(v_send, v_recv, K_V, c, range(per_blk))

    blocks(4, place_more, nth)
    to_pts(lambda peer: g_send.at[peer], g_recv, K_G)
    v_recv[me] = v_send[me]
    g_recv[me] = g_send[me]

    fetches[6].wait()
    index_col = jnp.broadcast_to(index, (LANES, points)).T
    lane = lax.broadcasted_iota(jnp.int32, (points, LANES), 1).astype(F32)
    for t in range(slots // LANES):
        pick[:, t * LANES : (t + 1) * LANES] = jnp.where(
            index_col == lane + t * LANES, 1.0, 0.0
        ).astype(BF16)
    normed_t[...] = nm.astype(F32).T.astype(BF16)
    gout_t[...] = gout_ref[...].astype(F32).T.astype(BF16)
    gk_part[:, KB] = jnp.zeros((NBLK, BLK, LANES), F32)
    gv_part[:, KB] = jnp.zeros((NBLK, BLK, LANES), F32)

    head_lane = lax.broadcasted_iota(jnp.int32, (BLK, LANES), 1) < HALF
    head_sub = lax.broadcasted_iota(jnp.int32, (LANES, BLK), 0) < HALF

    def block_of(ref, b, first=0):
        return ref[pl.ds(b * per_blk, per_blk), :, first : first + LANES].reshape(BLK, LANES)

    def halves(ref, b, rows):
        ref[b, 0:BLK] = jnp.where(head_lane, rows, 0.0).astype(BF16)
        ref[b, BLK : 2 * BLK] = jnp.where(head_lane, 0.0, rows).astype(BF16)

    def chosen_of(b):
        return [pat_ref[j, b] for j in range(KB)]

    wait_bytes(kq_recv.at[pl.ds(0, n - 1)], rsem.at[K_Q])

    def prepare(some):
        for b in some:
            q = block_of(kq_recv, b, LANES).astype(F32)
            empty = q > EMPTY_CUT
            bias[b] = jnp.where(empty, LOW, 0.0)
            halves(qs, b, jnp.where(empty, 0.0, q))
            k_t[b] = block_of(kq_recv, b).astype(F32).T.astype(BF16)

    blocks(8, prepare)

    def softmax(some):
        scores = []
        for b in some:
            chosen = chosen_of(b)
            keys = jnp.concatenate([block_of(kq_recv, c) for c in chosen], 0)
            low = jnp.concatenate([bias[c] for c in chosen], 0)
            scores.append(nt(keys, qs[b]) + jnp.concatenate([low, low], 1))
        for b, score in zip(some, scores):
            raised = jnp.exp(score - jnp.max(score, 0, keepdims=True))
            p = raised * (1.0 / jnp.sum(raised, 0, keepdims=True))
            probs[b] = p.astype(BF16)

    blocks(8, softmax)

    wait_bytes(v_recv.at[pl.ds(0, n - 1)], rsem.at[K_V])

    def prepare_v(some):
        for b in some:
            v_t[b] = block_of(v_recv, b).astype(F32).T.astype(BF16)

    blocks(8, prepare_v)

    def mix(some):
        ctx_t = [
            nn(jnp.concatenate([v_t[c] for c in chosen_of(b)], 1), probs[b]) for b in some
        ]
        ctx = [jnp.where(head_sub, c[:, 0:BLK], c[:, BLK : 2 * BLK]).T.astype(BF16) for c in ctx_t]
        for b, c in zip(some, ctx):
            ra_send[pl.ds(b * per_blk, per_blk)] = c.reshape(per_blk, cap, LANES)
        for b in some:
            to_group(ra_send, ra_recv, K_CTX, b, range(per_blk))

    blocks(8, mix, nth)
    ra_recv[me] = ra_send[me]

    wait_bytes(g_recv.at[pl.ds(0, n - 1)], rsem.at[K_G])

    def prepare_g(some):
        for b in some:
            halves(gs, b, block_of(g_recv, b).astype(F32))

    blocks(8, prepare_g)

    def interleave(b, first, count):
        for j in range(3):
            some = stack[b, pl.ds(3 * cap * first + j, cap * count, stride=3), :]
            rb_send[j, pl.ds(b * per_blk + first, count)] = some.astype(BF16).reshape(
                count, cap, LANES
            )

    def grads_of(some):
        dps = [
            nt(jnp.concatenate([block_of(v_recv, c) for c in chosen_of(b)], 0), gs[b])
            for b in some
        ]
        dss = []
        for b, dp in zip(some, dps):
            gv_part[b, 0:KB] = nn(probs[b], gs[b]).reshape(KB, BLK, LANES)
            p = probs[b].astype(F32)
            delta = jnp.sum(p * dp, 0, keepdims=True)
            dss.append((p * (dp - delta)).astype(BF16))
        gqs = []
        for b, ds in zip(some, dss):
            gq_t = nn(jnp.concatenate([k_t[c] for c in chosen_of(b)], 1), ds)
            gk_part[b, 0:KB] = nn(ds, qs[b]).reshape(KB, BLK, LANES)
            gqs.append(jnp.where(head_sub, gq_t[:, 0:BLK], gq_t[:, BLK : 2 * BLK]).T * 0.125)
        for b, gq in zip(some, gqs):
            stack[b, 0:BLK] = gq
        for b in some:
            interleave(b, 0, 1)
        for b in some:
            for j in range(3):
                to_group(rb_send.at[j], rb_recv.at[j], K_BACK + j, b, range(1))

    blocks(8, grads_of, nth)

    def key_side(some):
        for c in some:
            gk = jnp.zeros((BLK, LANES), F32)
            gv = jnp.zeros((BLK, LANES), F32)
            for b in range(NBLK):
                j = jnp.int32(KB)
                for which in range(KB):
                    j = jnp.where(pat_ref[which, b] == c, which, j)
                gk = gk + gk_part[b, j]
                gv = gv + gv_part[b, j]
            stack[c, BLK : 2 * BLK] = gk
            stack[c, 2 * BLK : 3 * BLK] = gv
        for c in some:
            interleave(c, 1, per_blk - 1)
        for c in some:
            to_group(rb_send.at[0], rb_recv.at[0], K_BACK, c, range(1, per_blk))

    blocks(8, key_side, nth)

    def send_slab(j):
        def one(i, carry):
            to_group(rb_send.at[j], rb_recv.at[j], K_BACK + j, nth(i), range(1, per_blk))
            return carry

        lax.fori_loop(0, NBLK, one, 0)

    send_slab(1)
    send_slab(2)
    for j in range(3):
        rb_recv[j, me] = rb_send[j, me]

    wait_bytes(ra_recv.at[pl.ds(0, n - 1)], rsem.at[K_CTX])
    context = nn(pick[...], ra_recv[...].reshape(slots, LANES)).astype(BF16)
    c_send[...] = context.reshape(tp, chunk, LANES)
    to_tp(lambda peer: c_send.at[peer], lambda at: c_recv.at[at], K_UPD)

    pair(3, nn(gout_t[...], c_send[...].reshape(points, LANES)).astype(BF16))
    c_recv[tm] = c_send[tm]
    wait_bytes(wo_all.at[pl.ds(0, tp - 1)], rsem.at[K_WO])
    wait_bytes(c_recv.at[pl.ds(0, tp - 1)], rsem.at[K_UPD])
    mine = pl.ds(pl.multiple_of(tm * chunk, chunk), chunk)
    update = sum(nn(c_recv[t], wo_all[t]) for t in range(tp)).astype(BF16).astype(F32)
    o_all[tm] = (pts_ref[mine, :].astype(F32) + update).astype(BF16)
    out_parts = ((K_OUT, pl.ds(0, chunk // 2)), (K_OUT_REST, pl.ds(chunk // 2, chunk // 2)))

    def send_out(which):
        phase, part = out_parts[which]
        to_tp(lambda peer: o_all.at[tm, part], lambda at: o_all.at[at, part], phase)

    wait_bytes(wqkv_all.at[pl.ds(0, tp - 1)], rsem.at[K_WQKV])

    acc[...] = jnp.zeros_like(acc)

    def add_rows(j):
        n_recv[j, tm] = n_send[j, tm]
        wait_bytes(n_recv.at[j, pl.ds(0, tp - 1)], rsem.at[K_N + j])
        acc[...] += sum(nt(n_recv[j, t], wqkv_all[t, j]) for t in range(tp))

    for j in range(3):
        wait_bytes(rb_recv.at[j, pl.ds(0, n - 1)], rsem.at[K_BACK + j])
        rows = nn(pick[...], rb_recv[j].reshape(slots, LANES)).astype(BF16)
        n_send[j] = rows.reshape(tp, chunk, LANES)
        to_tp(lambda peer: n_send.at[j, peer], lambda at: n_recv.at[j, at], K_N + j)
        if j != 1:
            send_out(j // 2)
        gw = nn(normed_t[...], rows)
        pair(j, gw.astype(BF16))
        weighted = gw * wqkv_all[tm, j].astype(F32)
        acc_gain[...] = weighted if j == 0 else acc_gain[...] + weighted
    gain_part = jnp.sum(acc_gain[...].T, 0, keepdims=True) / gain_ref[...]
    for j in range(width // LANES):
        gg_own[j] = gain_part[:, j * LANES : (j + 1) * LANES]
    remote(gg_own, gg_twin, K_GAIN_PAIR, twin).start()
    for which in (3, 0, 1, 2):
        fold(which)
    wait_bytes(gg_twin, rsem.at[K_GAIN_PAIR])
    gg_recv[my_chip] = gg_own[...] + gg_twin[...]
    to_chips(lambda chip: gg_recv.at[my_chip], gg_recv, K_GAIN)
    to_chips(lambda chip: gw_send.at[chip], gw_recv, K_W)

    add_rows(0)
    add_rows(1)
    wait_bytes(gg_recv.at[pl.ds(0, chips - 1)], rsem.at[K_GAIN])
    gx_recv[tm] = jnp.sum(gg_recv[...], 0)
    to_tp(lambda peer: gx_recv.at[tm], lambda at: gx_recv.at[at], K_GAINX)
    add_rows(2)
    grad = acc[...]
    grad = grad.astype(BF16).astype(F32)
    hat = xhat[mine, :]
    scaled = grad * gain_ref[...]
    first = jnp.mean(scaled, -1, keepdims=True)
    second = jnp.mean(scaled * hat, -1, keepdims=True)
    branch = (inv_std[mine, :] * (scaled - first - hat * second)).astype(BF16).astype(F32)
    i_all[tm] = (gout_ref[mine, :].astype(F32) + branch).astype(BF16)
    to_tp(lambda peer: i_all.at[tm], lambda at: i_all.at[at], K_IN)

    gw_recv[my_chip] = gw_send[my_chip]
    wait_bytes(gw_recv.at[pl.ds(0, chips - 1)], rsem.at[K_W])
    gw_all[my_c, my_chip] = jnp.sum(gw_recv[...].astype(F32), 0).astype(BF16)
    to_chips(lambda chip: gw_all.at[my_c, my_chip], gw_all.at[my_c], K_WALL)

    def hand(src, dst, which):
        copy = pltpu.make_async_copy(src, dst, out_sem.at[which])
        copy.start()
        return copy

    for phase, part in out_parts:
        wait_bytes(o_all.at[pl.ds(0, tp - 1), part], rsem.at[phase])
    handed = [hand(o_all, out_hbm, 0)]

    for phase, buf in (
        (K_Q, kq_send),
        (K_V, v_send),
        (K_G, g_send),
        (K_CTX, ra_send),
        (K_BACK, rb_send.at[0]),
        (K_BACK + 1, rb_send.at[1]),
        (K_BACK + 2, rb_send.at[2]),
    ):
        wait_bytes(buf.at[pl.ds(0, n - 1)], ssem.at[phase])
    for phase, buf in (
        (K_WO, wo_all),
        (K_WQKV, wqkv_all),
        (K_UPD, c_send),
        (K_N, n_send.at[0]),
        (K_N + 1, n_send.at[1]),
        (K_N + 2, n_send.at[2]),
    ):
        wait_bytes(buf.at[pl.ds(0, tp - 1)], ssem.at[phase])

    wait_bytes(gw_all.at[my_c, pl.ds(0, chips - 1)], rsem.at[K_WALL])
    remote(gw_all.at[my_c], gw_all.at[my_c], K_FORWARD, twin).start()
    for phase, part in out_parts:
        wait_bytes(o_all.at[pl.ds(0, tp - 1), part], ssem.at[phase])
    wait_bytes(gx_recv.at[pl.ds(0, tp - 1)], rsem.at[K_GAINX])
    gain_sum = jnp.sum(gx_recv[...], 0)
    for j in range(width // LANES):
        gain_out[:, j * LANES : (j + 1) * LANES] = gain_sum[j]
    handed.append(hand(gain_out, ggain_hbm, 1))
    wait_bytes(i_all.at[pl.ds(0, tp - 1)], rsem.at[K_IN])
    handed.append(hand(i_all, gin_hbm, 2))
    wait_bytes(gw_all.at[1 - my_c], rsem.at[K_FORWARD])
    handed.append(hand(gw_all, gw_hbm, 3))
    for phase, buf in ((K_IN, i_all), (K_GAINX, gx_recv)):
        wait_bytes(buf.at[pl.ds(0, tp - 1)], ssem.at[phase])
    wait_bytes(gg_own, ssem.at[K_GAIN_PAIR])
    wait_bytes(gg_recv.at[pl.ds(0, chips - 1)], ssem.at[K_GAIN])
    wait_bytes(gw_send.at[pl.ds(0, chips - 1)], ssem.at[K_W])
    wait_bytes(gw_all.at[my_c, pl.ds(0, chips - 1)], ssem.at[K_WALL])
    wait_bytes(gw_all.at[my_c], ssem.at[K_FORWARD])
    for which in range(4):
        wait_bytes(pair_recv.at[which], ssem.at[K_PAIR + which])
    for copy in handed:
        copy.wait()


def hand_out(
    out_in,
    gin_in,
    gw_in,
    gain_in,
    out_ref,
    gin_ref,
    gqkv_ref,
    gproj_ref,
    gain_ref,
    out_buf,
    gin_buf,
    gw_buf,
    gain_buf,
    gqkv_buf,
    gproj_buf,
    sems,
):
    def copy(src, dst, which):
        one = pltpu.make_async_copy(src, dst, sems.at[which])
        one.start()
        return one

    rows, width = out_buf.shape
    gw_get = copy(gw_in, gw_buf, 0)
    halves = []
    for i, (src, buf, dst) in enumerate(
        ((out_in, out_buf, out_ref), (gin_in, gin_buf, gin_ref))
    ):
        for k in range(2):
            part = pl.ds(k * rows // 2, rows // 2)
            get = copy(src.at[part], buf.at[part], 1 + 2 * i + k)
            halves.append((get, buf.at[part], dst.at[part], 5 + 2 * i + k))
    gain_get = copy(gain_in, gain_buf, 9)

    def whole(which):
        return gw_buf[:, :, which].reshape(width, LANES).astype(F32)

    puts = []
    gw_get.wait()
    for j in range(3):
        gqkv_buf[j] = whole(j)
    puts.append(copy(gqkv_buf, gqkv_ref, 10))
    for get, src, dst, sem in halves:
        get.wait()
        puts.append(copy(src, dst, sem))
    gproj_buf[...] = whole(3).T
    puts.append(copy(gproj_buf, gproj_ref, 11))
    gain_get.wait()
    puts.append(copy(gain_buf, gain_ref, 12))
    for put in puts:
        put.wait()


def body(n, tp, points, destination, pattern, norm_gain, qkv_weight, out_weight, grad_out):
    rows, width = points.shape
    cap = 2 * rows // n
    slots = n * cap
    chunk = rows // tp
    hbm = pl.BlockSpec(memory_space=pltpu.HBM)
    scratch = [
        pltpu.VMEM((rows, width), BF16),
        pltpu.VMEM((1, rows), jnp.int32),
        pltpu.SMEM((KB, NBLK), jnp.int32),
        pltpu.VMEM((1, width), F32),
        pltpu.VMEM((tp, 3, width, LANES), BF16),
        pltpu.VMEM((tp, LANES, width), BF16),
        pltpu.VMEM((rows, width), BF16),
        pltpu.SemaphoreType.DMA((7,)),
        pltpu.SemaphoreType.DMA((4,)),
        pltpu.VMEM((rows, width), F32),
        pltpu.VMEM((rows, 1), F32),
        pltpu.VMEM((rows, width), BF16),
        pltpu.VMEM((width, rows), BF16),
        pltpu.VMEM((width, rows), BF16),
        pltpu.VMEM((rows, slots), BF16),
        pltpu.VMEM((NBLK, BLK, rows), BF16),
        pltpu.VMEM((rows, 2 * LANES), BF16),
        pltpu.VMEM((rows, 2 * LANES), BF16),
        pltpu.VMEM((n, cap, 2 * LANES), BF16),
        pltpu.VMEM((n, cap, 2 * LANES), BF16),
        pltpu.VMEM((n, cap, LANES), BF16),
        pltpu.VMEM((n, cap, LANES), BF16),
        pltpu.VMEM((n, cap, LANES), BF16),
        pltpu.VMEM((n, cap, LANES), BF16),
        pltpu.VMEM((NBLK, 2 * BLK, LANES), BF16),
        pltpu.VMEM((NBLK, 2 * BLK, LANES), BF16),
        pltpu.VMEM((NBLK, LANES, BLK), BF16),
        pltpu.VMEM((NBLK, LANES, BLK), BF16),
        pltpu.VMEM((NBLK, BLK, LANES), F32),
        pltpu.VMEM((NBLK, KB * BLK, 2 * BLK), BF16),
        pltpu.VMEM((NBLK, KB + 1, BLK, LANES), F32),
        pltpu.VMEM((NBLK, KB + 1, BLK, LANES), F32),
        pltpu.VMEM((NBLK, 3 * BLK, LANES), F32),
        pltpu.VMEM((n, cap, LANES), BF16),
        pltpu.VMEM((n, cap, LANES), BF16),
        pltpu.VMEM((3, n, cap, LANES), BF16),
        pltpu.VMEM((3, n, cap, LANES), BF16),
        pltpu.VMEM((tp, chunk, LANES), BF16),
        pltpu.VMEM((tp, chunk, LANES), BF16),
        pltpu.VMEM((3, tp, chunk, LANES), BF16),
        pltpu.VMEM((3, tp, chunk, LANES), BF16),
        pltpu.VMEM((chunk, width), F32),
        pltpu.VMEM((width, LANES), F32),
        pltpu.VMEM((tp, chunk, width), BF16),
        pltpu.VMEM((tp, chunk, width), BF16),
        pltpu.VMEM((4, CORES, width // CORES, LANES), BF16),
        pltpu.VMEM((4, width // CORES, LANES), BF16),
        pltpu.VMEM((n // CORES, 4, width // n, LANES), BF16),
        pltpu.VMEM((n // CORES, 4, width // n, LANES), BF16),
        pltpu.VMEM((CORES, n // CORES, 4, width // n, LANES), BF16),
        pltpu.VMEM((width // LANES, 1, LANES), F32),
        pltpu.VMEM((width // LANES, 1, LANES), F32),
        pltpu.VMEM((n // CORES, width // LANES, 1, LANES), F32),
        pltpu.VMEM((tp, width // LANES, 1, LANES), F32),
        pltpu.VMEM((1, width), F32),
        pltpu.SemaphoreType.DMA((PHASES,)),
        pltpu.SemaphoreType.DMA((PHASES,)),
    ]
    out_shape = jax.ShapeDtypeStruct((rows, width), BF16)
    gain_shape = jax.ShapeDtypeStruct((1, width), F32)
    qkv_shape = jax.ShapeDtypeStruct((3, width, LANES), F32)
    proj_shape = jax.ShapeDtypeStruct((LANES, width), F32)
    by_tp = jax.ShapeDtypeStruct((tp, chunk, width), BF16)
    parts = jax.ShapeDtypeStruct((CORES, n // CORES, 4, width // n, LANES), BF16)
    out, grad_input, grads, gain = pl.pallas_call(
        functools.partial(kernel, n, tp),
        out_shape=(by_tp, by_tp, parts, gain_shape),
        in_specs=[hbm] * 7,
        out_specs=(hbm,) * 4,
        scratch_shapes=scratch,
        compiler_params=pltpu.CompilerParams(
            collective_id=0, has_side_effects=True, vmem_limit_bytes=VMEM_LIMIT
        ),
        name="point_attention",
    )(
        points,
        destination.reshape(1, rows),
        pattern.T,
        norm_gain.reshape(1, width),
        qkv_weight,
        out_weight,
        grad_out,
    )
    out, grad_input, grad_qkv, grad_proj, grad_gain = pl.pallas_call(
        hand_out,
        out_shape=(out_shape, out_shape, qkv_shape, proj_shape, gain_shape),
        in_specs=[hbm] * 4,
        out_specs=(hbm,) * 5,
        scratch_shapes=[
            pltpu.VMEM((rows, width), BF16),
            pltpu.VMEM((rows, width), BF16),
            pltpu.VMEM((CORES, n // CORES, 4, width // n, LANES), BF16),
            pltpu.VMEM((1, width), F32),
            pltpu.VMEM((3, width, LANES), F32),
            pltpu.VMEM((LANES, width), F32),
            pltpu.SemaphoreType.DMA((13,)),
        ],
        compiler_params=pltpu.CompilerParams(vmem_limit_bytes=VMEM_LIMIT),
        name="hand_out",
    )(out.reshape(rows, width), grad_input.reshape(rows, width), grads, gain)
    return out, grad_input, grad_qkv, grad_proj, grad_gain.reshape(width)


def solution(mesh):
    return jax.shard_map(
        functools.partial(body, mesh.shape["pts"], mesh.shape["tp"]),
        mesh=mesh,
        in_specs=(
            P("pts", None),
            P("pts", None),
            P("pts", None),
            P(),
            P(None, None, "tp"),
            P("tp", None),
            P("pts", None),
        ),
        out_specs=(P("pts", None), P("pts", None), P(None, None, "tp"), P("tp", None), P()),
        check_vma=False,
    )
```

```python
import functools

import jax
import jax.numpy as jnp
from jax import lax
from jax.experimental import pallas as pl
from jax.experimental.pallas import tpu as pltpu
from jax.sharding import PartitionSpec as P

MESH = pl.DeviceIdType.MESH
F32 = jnp.float32
BF16 = jnp.bfloat16
BLK = 128
NBLK = 8
KB = 4
LANES = 128
HALF = 64
EMPTY = 2e38
EMPTY_CUT = 1e38
LOW = -1e30
VMEM_LIMIT = 60 * 1024 * 1024
YS, ZS, CORES = 4, 4, 2


def ring(step, size):
    return min(step, size - step)


OFFSETS = sorted(
    [(y, z, c) for y in range(YS) for z in range(ZS) for c in range(CORES)][1:],
    key=lambda o: (-ring(o[0], YS) - ring(o[1], ZS), o),
)

CHIPS = [(y, z) for y, z, c in OFFSETS if c == 0]

(K_Q, K_V, K_G, K_CTX, K_BACK, K_UPD, K_OUT, K_N, K_IN, K_W, K_GAIN, K_GAINX, K_WO, K_WQKV) = (
    0, 1, 2, 3, 4, 7, 8, 9, 12, 13, 15, 16, 17, 18
)
K_PAIR, K_FORWARD, K_OUT_REST, K_GAIN_PAIR, K_CHIPS, PHASES = 19, 26, 24, 25, 28, 30


def nn(a, b):
    return jnp.dot(a, b, preferred_element_type=F32)


def nt(a, b):
    return lax.dot_general(a, b, (((1,), (1,)), ((), ())), preferred_element_type=F32)


def wait_bytes(ref, sem):
    pltpu.make_async_copy(ref, ref, sem).wait()


def kernel(
    n,
    tp,
    pts_hbm,
    dest_hbm,
    pat_hbm,
    gain_hbm,
    wqkv_hbm,
    wo_hbm,
    gout_hbm,
    out_hbm,
    gin_hbm,
    gw_hbm,
    ggain_hbm,
    pts_ref,
    dest_ref,
    pat_ref,
    gain_ref,
    wqkv_all,
    wo_all,
    gout_ref,
    in_sem,
    out_sem,
    xhat,
    inv_std,
    normed,
    normed_t,
    gout_t,
    pick,
    put_all,
    rows_kq,
    rows_vg,
    kq_send,
    kq_recv,
    v_send,
    v_recv,
    g_send,
    g_recv,
    qs,
    gs,
    k_t,
    v_t,
    bias,
    probs,
    gk_part,
    gv_part,
    stack,
    ra_send,
    ra_recv,
    rb_send,
    rb_recv,
    c_send,
    c_recv,
    n_send,
    n_recv,
    acc,
    acc_gain,
    o_all,
    i_all,
    pair_send,
    pair_recv,
    gw_send,
    gw_recv,
    gw_all,
    gg_own,
    gg_twin,
    gg_recv,
    gx_recv,
    gain_out,
    ssem,
    rsem,
):
    me = lax.axis_index("pts")
    tm = lax.axis_index("tp")
    cap = kq_send.shape[1]
    per_blk = BLK // cap
    points, width = pts_ref.shape
    slots = n * cap
    chunk = points // tp
    my_y = me // (ZS * CORES)
    my_z = lax.rem(me // CORES, ZS)
    my_c = lax.rem(me, CORES)

    fetches = [
        pltpu.make_async_copy(src, dst, in_sem.at[i])
        for i, (src, dst) in enumerate(
            (
                (dest_hbm, dest_ref),
                (pts_hbm, pts_ref),
                (gain_hbm, gain_ref),
                (wqkv_hbm, wqkv_all.at[tm]),
                (gout_hbm, gout_ref),
                (wo_hbm, wo_all.at[tm]),
                (pat_hbm, pat_ref),
            )
        )
    ]
    for fetch in fetches:
        fetch.start()

    barrier = pltpu.get_barrier_semaphore()

    def greet(i, carry):
        pl.semaphore_signal(
            barrier, inc=1, device_id=(lax.rem(me + i, n), tm), device_id_type=MESH
        )
        return carry

    for i in range(1, tp):
        pl.semaphore_signal(
            barrier, inc=1, device_id=(me, lax.rem(tm + i, tp)), device_id_type=MESH
        )
    lax.fori_loop(1, n, greet, 0)

    def remote(src, dst, phase, peer):
        return pltpu.make_async_remote_copy(
            src_ref=src,
            dst_ref=dst,
            send_sem=ssem.at[phase],
            recv_sem=rsem.at[phase],
            device_id=peer,
            device_id_type=MESH,
        )

    def to_pts(send, recv, phase):
        for dy, dz, dc in OFFSETS:
            peer = (lax.rem(my_y + dy, YS) * ZS + lax.rem(my_z + dz, ZS)) * CORES
            peer = peer + lax.rem(my_c + dc, CORES)
            remote(send(peer), recv.at[me], phase, (peer, tm)).start()

    chips = n // CORES
    my_chip = me // CORES
    twin = (me + 1 - 2 * my_c, tm)

    def to_chips(send, recv, phase):
        for dy, dz in CHIPS:
            chip = lax.rem(my_y + dy, YS) * ZS + lax.rem(my_z + dz, ZS)
            remote(send(chip), recv.at[my_chip], phase, (chip * CORES + my_c, tm)).start()

    def pair(which, rows):
        pair_send[which] = rows.reshape(pair_send.shape[1:])
        remote(
            pair_send.at[which, 1 - my_c], pair_recv.at[which], K_PAIR + which, twin
        ).start()

    def fold(which):
        wait_bytes(pair_recv.at[which], rsem.at[K_PAIR + which])
        both = pair_send[which, my_c].astype(F32) + pair_recv[which].astype(F32)
        gw_send[:, which] = both.astype(BF16).reshape(chips, width // n, LANES)

    def to_tp(send, recv, phase):
        for i in range(1, tp):
            peer = lax.rem(tm + i, tp)
            remote(send(peer), recv(tm), phase, (me, peer)).start()

    def nth(i):
        dy = jnp.where(i < 2, 2, jnp.where(i < 6, 1 + 2 * lax.rem(i, 2), 0))
        dz = jnp.where(i < 2, 1 - i, jnp.where(i < 6, 1 - (i - 2) // 2, 7 - i))
        return lax.rem(my_y + dy, YS) * 2 + lax.rem(my_z // 2 + dz, 2)

    def blocks(step, work, order=None):
        def some(i, carry):
            at = [i * step + k for k in range(step)]
            work([order(a) for a in at] if order else at)
            return carry

        lax.fori_loop(0, NBLK // step, some, 0)

    def to_group(send, recv, phase, b, which):
        for u in which:
            peer = b * per_blk + u

            @pl.when(peer != me)
            def _():
                remote(send.at[peer], recv.at[me], phase, (peer, tm)).start()

    upto = jnp.where(
        lax.broadcasted_iota(jnp.int32, (points, points), 0)
        <= lax.broadcasted_iota(jnp.int32, (points, points), 1),
        1.0,
        0.0,
    ).astype(BF16)
    fetches[0].wait()
    dest = dest_ref[...].astype(F32)
    owner = lax.broadcasted_iota(jnp.int32, (n, points), 0).astype(F32)
    onehot = jnp.where(dest == owner, 1.0, 0.0)
    count = nn(onehot.astype(BF16), upto)
    index = dest * cap + jnp.sum(count * onehot, 0, keepdims=True) - 1.0

    fetches[1].wait()
    fetches[2].wait()

    for r in range(points // BLK):
        at = pl.ds(r * BLK, BLK)
        x = pts_ref[at, :].astype(F32)
        shifted = x - jnp.mean(x, -1, keepdims=True)
        inv = lax.rsqrt(jnp.mean(shifted * shifted, -1, keepdims=True) + 1e-05)
        hat = shifted * inv
        xhat[at, :] = hat
        inv_std[at, :] = inv
        normed[at, :] = (hat * gain_ref[...]).astype(BF16)

    fetches[3].wait()
    nm = normed[...]
    rows_kq[:, 0:LANES] = nn(nm, wqkv_all[tm, 1]).astype(BF16)
    rows_kq[:, LANES : 2 * LANES] = (nn(nm, wqkv_all[tm, 0]).astype(BF16).astype(F32) * 0.125).astype(
        BF16
    )
    slot_sub = lax.broadcasted_iota(jnp.int32, (BLK, points), 0).astype(F32)
    ones = jnp.ones((points, LANES), BF16)

    pl.semaphore_wait(barrier, n - 1 + tp - 1)

    def place(some):
        puts = [
            jnp.where(slot_sub + (c * BLK).astype(F32) == index, 1.0, 0.0).astype(BF16)
            for c in some
        ]
        lives = [nn(put, ones) for put in puts]
        kqs = [nn(put, rows_kq[...]) for put in puts]
        for c, put, live, kq in zip(some, puts, lives, kqs):
            put_all[c] = put
            k = kq[:, 0:LANES].astype(BF16)
            q = jnp.where(live > 0.5, kq[:, LANES : 2 * LANES], EMPTY).astype(BF16)
            at = pl.ds(c * per_blk, per_blk)
            kq_send[at, :, 0:LANES] = k.reshape(per_blk, cap, LANES)
            kq_send[at, :, LANES : 2 * LANES] = q.reshape(per_blk, cap, LANES)
        for c in some:
            to_group(kq_send, kq_recv, K_Q, c, range(per_blk))

    blocks(2, place, nth)
    kq_recv[me] = kq_send[me]

    fetches[4].wait()
    fetches[5].wait()
    to_tp(lambda peer: wo_all.at[tm], lambda at: wo_all.at[at], K_WO)
    to_tp(lambda peer: wqkv_all.at[tm], lambda at: wqkv_all.at[at], K_WQKV)
    rows_vg[:, 0:LANES] = nn(nm, wqkv_all[tm, 2]).astype(BF16)
    rows_vg[:, LANES : 2 * LANES] = nt(gout_ref[...], wo_all[tm]).astype(BF16)

    def place_more(some):
        vgs = [nn(put_all[c], rows_vg[...]).astype(BF16) for c in some]
        for c, vg in zip(some, vgs):
            at = pl.ds(c * per_blk, per_blk)
            v_send[at] = vg[:, 0:LANES].reshape(per_blk, cap, LANES)
            g_send[at] = vg[:, LANES : 2 * LANES].reshape(per_blk, cap, LANES)
        for c in some:
            to_group(v_send, v_recv, K_V, c, range(per_blk))

    blocks(4, place_more, nth)
    to_pts(lambda peer: g_send.at[peer], g_recv, K_G)
    v_recv[me] = v_send[me]
    g_recv[me] = g_send[me]

    fetches[6].wait()
    index_col = jnp.broadcast_to(index, (LANES, points)).T
    lane = lax.broadcasted_iota(jnp.int32, (points, LANES), 1).astype(F32)
    for t in range(slots // LANES):
        pick[:, t * LANES : (t + 1) * LANES] = jnp.where(
            index_col == lane + t * LANES, 1.0, 0.0
        ).astype(BF16)
    normed_t[...] = nm.astype(F32).T.astype(BF16)
    gout_t[...] = gout_ref[...].astype(F32).T.astype(BF16)
    gk_part[:, KB] = jnp.zeros((NBLK, BLK, LANES), F32)
    gv_part[:, KB] = jnp.zeros((NBLK, BLK, LANES), F32)

    head_lane = lax.broadcasted_iota(jnp.int32, (BLK, LANES), 1) < HALF
    head_sub = lax.broadcasted_iota(jnp.int32, (LANES, BLK), 0) < HALF

    def block_of(ref, b, first=0):
        return ref[pl.ds(b * per_blk, per_blk), :, first : first + LANES].reshape(BLK, LANES)

    def halves(ref, b, rows):
        ref[b, 0:BLK] = jnp.where(head_lane, rows, 0.0).astype(BF16)
        ref[b, BLK : 2 * BLK] = jnp.where(head_lane, 0.0, rows).astype(BF16)

    def chosen_of(b):
        return [pat_ref[j, b] for j in range(KB)]

    wait_bytes(kq_recv.at[pl.ds(0, n - 1)], rsem.at[K_Q])

    def prepare(some):
        for b in some:
            q = block_of(kq_recv, b, LANES).astype(F32)
            empty = q > EMPTY_CUT
            bias[b] = jnp.where(empty, LOW, 0.0)
            halves(qs, b, jnp.where(empty, 0.0, q))
            k_t[b] = block_of(kq_recv, b).astype(F32).T.astype(BF16)

    blocks(8, prepare)

    def softmax(some):
        scores = []
        for b in some:
            chosen = chosen_of(b)
            keys = jnp.concatenate([block_of(kq_recv, c) for c in chosen], 0)
            low = jnp.concatenate([bias[c] for c in chosen], 0)
            scores.append(nt(keys, qs[b]) + jnp.concatenate([low, low], 1))
        for b, score in zip(some, scores):
            raised = jnp.exp(score - jnp.max(score, 0, keepdims=True))
            p = raised * (1.0 / jnp.sum(raised, 0, keepdims=True))
            probs[b] = p.astype(BF16)

    blocks(8, softmax)

    wait_bytes(v_recv.at[pl.ds(0, n - 1)], rsem.at[K_V])

    def prepare_v(some):
        for b in some:
            v_t[b] = block_of(v_recv, b).astype(F32).T.astype(BF16)

    blocks(8, prepare_v)

    def mix(some):
        ctx_t = [
            nn(jnp.concatenate([v_t[c] for c in chosen_of(b)], 1), probs[b]) for b in some
        ]
        ctx = [jnp.where(head_sub, c[:, 0:BLK], c[:, BLK : 2 * BLK]).T.astype(BF16) for c in ctx_t]
        for b, c in zip(some, ctx):
            ra_send[pl.ds(b * per_blk, per_blk)] = c.reshape(per_blk, cap, LANES)
        for b in some:
            to_group(ra_send, ra_recv, K_CTX, b, range(per_blk))

    blocks(8, mix, nth)
    ra_recv[me] = ra_send[me]

    wait_bytes(g_recv.at[pl.ds(0, n - 1)], rsem.at[K_G])

    def prepare_g(some):
        for b in some:
            halves(gs, b, block_of(g_recv, b).astype(F32))

    blocks(8, prepare_g)

    def interleave(b, first, count):
        for j in range(3):
            some = stack[b, pl.ds(3 * cap * first + j, cap * count, stride=3), :]
            rb_send[j, pl.ds(b * per_blk + first, count)] = some.astype(BF16).reshape(
                count, cap, LANES
            )

    def grads_of(some):
        dps = [
            nt(jnp.concatenate([block_of(v_recv, c) for c in chosen_of(b)], 0), gs[b])
            for b in some
        ]
        dss = []
        for b, dp in zip(some, dps):
            gv_part[b, 0:KB] = nn(probs[b], gs[b]).reshape(KB, BLK, LANES)
            p = probs[b].astype(F32)
            delta = jnp.sum(p * dp, 0, keepdims=True)
            dss.append((p * (dp - delta)).astype(BF16))
        gqs = []
        for b, ds in zip(some, dss):
            gq_t = nn(jnp.concatenate([k_t[c] for c in chosen_of(b)], 1), ds)
            gk_part[b, 0:KB] = nn(ds, qs[b]).reshape(KB, BLK, LANES)
            gqs.append(jnp.where(head_sub, gq_t[:, 0:BLK], gq_t[:, BLK : 2 * BLK]).T * 0.125)
        for b, gq in zip(some, gqs):
            stack[b, 0:BLK] = gq
        for b in some:
            interleave(b, 0, 1)
        for b in some:
            for j in range(3):
                to_group(rb_send.at[j], rb_recv.at[j], K_BACK + j, b, range(1))

    blocks(8, grads_of, nth)

    def key_side(some):
        for c in some:
            gk = jnp.zeros((BLK, LANES), F32)
            gv = jnp.zeros((BLK, LANES), F32)
            for b in range(NBLK):
                j = jnp.int32(KB)
                for which in range(KB):
                    j = jnp.where(pat_ref[which, b] == c, which, j)
                gk = gk + gk_part[b, j]
                gv = gv + gv_part[b, j]
            stack[c, BLK : 2 * BLK] = gk
            stack[c, 2 * BLK : 3 * BLK] = gv
        for c in some:
            interleave(c, 1, per_blk - 1)
        for c in some:
            to_group(rb_send.at[0], rb_recv.at[0], K_BACK, c, range(1, per_blk))

    blocks(4, key_side, nth)

    def send_slab(j):
        def one(i, carry):
            to_group(rb_send.at[j], rb_recv.at[j], K_BACK + j, nth(i), range(1, per_blk))
            return carry

        lax.fori_loop(0, NBLK, one, 0)

    send_slab(1)
    send_slab(2)
    for j in range(3):
        rb_recv[j, me] = rb_send[j, me]

    wait_bytes(ra_recv.at[pl.ds(0, n - 1)], rsem.at[K_CTX])
    context = nn(pick[...], ra_recv[...].reshape(slots, LANES)).astype(BF16)
    c_send[...] = context.reshape(tp, chunk, LANES)
    to_tp(lambda peer: c_send.at[peer], lambda at: c_recv.at[at], K_UPD)

    pair(3, nn(gout_t[...], c_send[...].reshape(points, LANES)).astype(BF16))
    c_recv[tm] = c_send[tm]
    wait_bytes(wo_all.at[pl.ds(0, tp - 1)], rsem.at[K_WO])
    wait_bytes(c_recv.at[pl.ds(0, tp - 1)], rsem.at[K_UPD])
    mine = pl.ds(pl.multiple_of(tm * chunk, chunk), chunk)
    update = sum(nn(c_recv[t], wo_all[t]) for t in range(tp)).astype(BF16).astype(F32)
    o_all[tm] = (pts_ref[mine, :].astype(F32) + update).astype(BF16)
    out_parts = ((K_OUT, pl.ds(0, chunk // 2)), (K_OUT_REST, pl.ds(chunk // 2, chunk // 2)))

    def send_out(which):
        phase, part = out_parts[which]
        to_tp(lambda peer: o_all.at[tm, part], lambda at: o_all.at[at, part], phase)

    send_out(0)
    wait_bytes(wqkv_all.at[pl.ds(0, tp - 1)], rsem.at[K_WQKV])

    acc[...] = jnp.zeros_like(acc)

    def add_rows(j):
        n_recv[j, tm] = n_send[j, tm]
        wait_bytes(n_recv.at[j, pl.ds(0, tp - 1)], rsem.at[K_N + j])
        acc[...] += sum(nt(n_recv[j, t], wqkv_all[t, j]) for t in range(tp))

    for j in range(3):
        wait_bytes(rb_recv.at[j, pl.ds(0, n - 1)], rsem.at[K_BACK + j])
        rows = nn(pick[...], rb_recv[j].reshape(slots, LANES)).astype(BF16)
        n_send[j] = rows.reshape(tp, chunk, LANES)
        to_tp(lambda peer: n_send.at[j, peer], lambda at: n_recv.at[j, at], K_N + j)
        if j == 2:
            send_out(1)
        gw = nn(normed_t[...], rows)
        pair(j, gw.astype(BF16))
        weighted = gw * wqkv_all[tm, j].astype(F32)
        acc_gain[...] = weighted if j == 0 else acc_gain[...] + weighted
    gain_part = jnp.sum(acc_gain[...].T, 0, keepdims=True) / gain_ref[...]
    for j in range(width // LANES):
        gg_own[j] = gain_part[:, j * LANES : (j + 1) * LANES]
    remote(gg_own, gg_twin, K_GAIN_PAIR, twin).start()
    for which in (3, 0, 1, 2):
        fold(which)
    wait_bytes(gg_twin, rsem.at[K_GAIN_PAIR])
    gg_recv[my_chip] = gg_own[...] + gg_twin[...]
    to_chips(lambda chip: gg_recv.at[my_chip], gg_recv, K_GAIN)
    to_chips(lambda chip: gw_send.at[chip], gw_recv, K_W)

    add_rows(0)
    add_rows(1)
    wait_bytes(gg_recv.at[pl.ds(0, chips - 1)], rsem.at[K_GAIN])
    gx_recv[tm] = jnp.sum(gg_recv[...], 0)
    to_tp(lambda peer: gx_recv.at[tm], lambda at: gx_recv.at[at], K_GAINX)
    add_rows(2)
    grad = acc[...]
    grad = grad.astype(BF16).astype(F32)
    hat = xhat[mine, :]
    scaled = grad * gain_ref[...]
    first = jnp.mean(scaled, -1, keepdims=True)
    second = jnp.mean(scaled * hat, -1, keepdims=True)
    branch = (inv_std[mine, :] * (scaled - first - hat * second)).astype(BF16).astype(F32)
    i_all[tm] = (gout_ref[mine, :].astype(F32) + branch).astype(BF16)
    to_tp(lambda peer: i_all.at[tm], lambda at: i_all.at[at], K_IN)

    part_chips = chips // 2
    gw_recv[my_chip] = gw_send[my_chip]
    wait_bytes(gw_recv.at[pl.ds(0, chips - 1)], rsem.at[K_W])
    gw_all[my_c, my_chip] = jnp.sum(gw_recv[...].astype(F32), 0).astype(BF16)
    to_chips(lambda chip: gw_all.at[my_c, my_chip], gw_all.at[my_c], K_CHIPS + my_chip // part_chips)

    def hand(src, dst, which):
        copy = pltpu.make_async_copy(src, dst, out_sem.at[which])
        copy.start()
        return copy

    for phase, part in out_parts:
        wait_bytes(o_all.at[pl.ds(0, tp - 1), part], rsem.at[phase])
    handed = [hand(o_all, out_hbm, 0)]

    for phase, buf in (
        (K_Q, kq_send),
        (K_V, v_send),
        (K_G, g_send),
        (K_CTX, ra_send),
        (K_BACK, rb_send.at[0]),
        (K_BACK + 1, rb_send.at[1]),
        (K_BACK + 2, rb_send.at[2]),
    ):
        wait_bytes(buf.at[pl.ds(0, n - 1)], ssem.at[phase])
    for phase, buf in (
        (K_WO, wo_all),
        (K_WQKV, wqkv_all),
        (K_UPD, c_send),
        (K_N, n_send.at[0]),
        (K_N + 1, n_send.at[1]),
        (K_N + 2, n_send.at[2]),
    ):
        wait_bytes(buf.at[pl.ds(0, tp - 1)], ssem.at[phase])

    for h in range(2):

        @pl.when(my_chip // part_chips == h)
        def _():
            wait_bytes(gw_all.at[my_c, pl.ds(0, part_chips - 1)], rsem.at[K_CHIPS + h])

        @pl.when(my_chip // part_chips != h)
        def _():
            wait_bytes(gw_all.at[my_c, pl.ds(0, part_chips)], rsem.at[K_CHIPS + h])

        some = gw_all.at[my_c, pl.ds(h * part_chips, part_chips)]
        remote(some, some, K_FORWARD + h, twin).start()
    for phase, part in out_parts:
        wait_bytes(o_all.at[pl.ds(0, tp - 1), part], ssem.at[phase])
    wait_bytes(gx_recv.at[pl.ds(0, tp - 1)], rsem.at[K_GAINX])
    gain_sum = jnp.sum(gx_recv[...], 0)
    for j in range(width // LANES):
        gain_out[:, j * LANES : (j + 1) * LANES] = gain_sum[j]
    handed.append(hand(gain_out, ggain_hbm, 1))
    wait_bytes(i_all.at[pl.ds(0, tp - 1)], rsem.at[K_IN])
    handed.append(hand(i_all, gin_hbm, 2))
    for h in range(2):
        wait_bytes(gw_all.at[1 - my_c, pl.ds(h * part_chips, part_chips)], rsem.at[K_FORWARD + h])
    handed.append(hand(gw_all, gw_hbm, 3))
    for phase, buf in ((K_IN, i_all), (K_GAINX, gx_recv)):
        wait_bytes(buf.at[pl.ds(0, tp - 1)], ssem.at[phase])
    wait_bytes(gg_own, ssem.at[K_GAIN_PAIR])
    wait_bytes(gg_recv.at[pl.ds(0, chips - 1)], ssem.at[K_GAIN])
    wait_bytes(gw_send.at[pl.ds(0, chips - 1)], ssem.at[K_W])
    wait_bytes(gw_all.at[my_c, pl.ds(0, chips - 1)], ssem.at[K_CHIPS + my_chip // part_chips])
    for h in range(2):
        wait_bytes(gw_all.at[my_c, pl.ds(h * part_chips, part_chips)], ssem.at[K_FORWARD + h])
    for which in range(4):
        wait_bytes(pair_recv.at[which], ssem.at[K_PAIR + which])
    for copy in handed:
        copy.wait()


def hand_out(
    out_in,
    gin_in,
    gw_in,
    gain_in,
    out_ref,
    gin_ref,
    gqkv_ref,
    gproj_ref,
    gain_ref,
    out_buf,
    gin_buf,
    gw_buf,
    gain_buf,
    gqkv_buf,
    gproj_buf,
    sems,
):
    def copy(src, dst, which):
        one = pltpu.make_async_copy(src, dst, sems.at[which])
        one.start()
        return one

    rows, width = out_buf.shape
    gw_get = copy(gw_in, gw_buf, 0)
    halves = []
    for i, (src, buf, dst) in enumerate(
        ((out_in, out_buf, out_ref), (gin_in, gin_buf, gin_ref))
    ):
        for k in range(2):
            part = pl.ds(k * rows // 2, rows // 2)
            get = copy(src.at[part], buf.at[part], 1 + 2 * i + k)
            halves.append((get, buf.at[part], dst.at[part], 5 + 2 * i + k))
    gain_get = copy(gain_in, gain_buf, 9)

    def whole(which):
        return gw_buf[:, :, which].reshape(width, LANES).astype(F32)

    puts = []
    gw_get.wait()
    for j in range(3):
        gqkv_buf[j] = whole(j)
    puts.append(copy(gqkv_buf, gqkv_ref, 10))
    for get, src, dst, sem in halves:
        get.wait()
        puts.append(copy(src, dst, sem))
    gproj_buf[...] = whole(3).T
    puts.append(copy(gproj_buf, gproj_ref, 11))
    gain_get.wait()
    puts.append(copy(gain_buf, gain_ref, 12))
    for put in puts:
        put.wait()


def body(n, tp, points, destination, pattern, norm_gain, qkv_weight, out_weight, grad_out):
    rows, width = points.shape
    cap = 2 * rows // n
    slots = n * cap
    chunk = rows // tp
    hbm = pl.BlockSpec(memory_space=pltpu.HBM)
    scratch = [
        pltpu.VMEM((rows, width), BF16),
        pltpu.VMEM((1, rows), jnp.int32),
        pltpu.SMEM((KB, NBLK), jnp.int32),
        pltpu.VMEM((1, width), F32),
        pltpu.VMEM((tp, 3, width, LANES), BF16),
        pltpu.VMEM((tp, LANES, width), BF16),
        pltpu.VMEM((rows, width), BF16),
        pltpu.SemaphoreType.DMA((7,)),
        pltpu.SemaphoreType.DMA((4,)),
        pltpu.VMEM((rows, width), F32),
        pltpu.VMEM((rows, 1), F32),
        pltpu.VMEM((rows, width), BF16),
        pltpu.VMEM((width, rows), BF16),
        pltpu.VMEM((width, rows), BF16),
        pltpu.VMEM((rows, slots), BF16),
        pltpu.VMEM((NBLK, BLK, rows), BF16),
        pltpu.VMEM((rows, 2 * LANES), BF16),
        pltpu.VMEM((rows, 2 * LANES), BF16),
        pltpu.VMEM((n, cap, 2 * LANES), BF16),
        pltpu.VMEM((n, cap, 2 * LANES), BF16),
        pltpu.VMEM((n, cap, LANES), BF16),
        pltpu.VMEM((n, cap, LANES), BF16),
        pltpu.VMEM((n, cap, LANES), BF16),
        pltpu.VMEM((n, cap, LANES), BF16),
        pltpu.VMEM((NBLK, 2 * BLK, LANES), BF16),
        pltpu.VMEM((NBLK, 2 * BLK, LANES), BF16),
        pltpu.VMEM((NBLK, LANES, BLK), BF16),
        pltpu.VMEM((NBLK, LANES, BLK), BF16),
        pltpu.VMEM((NBLK, BLK, LANES), F32),
        pltpu.VMEM((NBLK, KB * BLK, 2 * BLK), BF16),
        pltpu.VMEM((NBLK, KB + 1, BLK, LANES), F32),
        pltpu.VMEM((NBLK, KB + 1, BLK, LANES), F32),
        pltpu.VMEM((NBLK, 3 * BLK, LANES), F32),
        pltpu.VMEM((n, cap, LANES), BF16),
        pltpu.VMEM((n, cap, LANES), BF16),
        pltpu.VMEM((3, n, cap, LANES), BF16),
        pltpu.VMEM((3, n, cap, LANES), BF16),
        pltpu.VMEM((tp, chunk, LANES), BF16),
        pltpu.VMEM((tp, chunk, LANES), BF16),
        pltpu.VMEM((3, tp, chunk, LANES), BF16),
        pltpu.VMEM((3, tp, chunk, LANES), BF16),
        pltpu.VMEM((chunk, width), F32),
        pltpu.VMEM((width, LANES), F32),
        pltpu.VMEM((tp, chunk, width), BF16),
        pltpu.VMEM((tp, chunk, width), BF16),
        pltpu.VMEM((4, CORES, width // CORES, LANES), BF16),
        pltpu.VMEM((4, width // CORES, LANES), BF16),
        pltpu.VMEM((n // CORES, 4, width // n, LANES), BF16),
        pltpu.VMEM((n // CORES, 4, width // n, LANES), BF16),
        pltpu.VMEM((CORES, n // CORES, 4, width // n, LANES), BF16),
        pltpu.VMEM((width // LANES, 1, LANES), F32),
        pltpu.VMEM((width // LANES, 1, LANES), F32),
        pltpu.VMEM((n // CORES, width // LANES, 1, LANES), F32),
        pltpu.VMEM((tp, width // LANES, 1, LANES), F32),
        pltpu.VMEM((1, width), F32),
        pltpu.SemaphoreType.DMA((PHASES,)),
        pltpu.SemaphoreType.DMA((PHASES,)),
    ]
    out_shape = jax.ShapeDtypeStruct((rows, width), BF16)
    gain_shape = jax.ShapeDtypeStruct((1, width), F32)
    qkv_shape = jax.ShapeDtypeStruct((3, width, LANES), F32)
    proj_shape = jax.ShapeDtypeStruct((LANES, width), F32)
    by_tp = jax.ShapeDtypeStruct((tp, chunk, width), BF16)
    parts = jax.ShapeDtypeStruct((CORES, n // CORES, 4, width // n, LANES), BF16)
    out, grad_input, grads, gain = pl.pallas_call(
        functools.partial(kernel, n, tp),
        out_shape=(by_tp, by_tp, parts, gain_shape),
        in_specs=[hbm] * 7,
        out_specs=(hbm,) * 4,
        scratch_shapes=scratch,
        compiler_params=pltpu.CompilerParams(
            collective_id=0, has_side_effects=True, vmem_limit_bytes=VMEM_LIMIT
        ),
        name="point_attention",
    )(
        points,
        destination.reshape(1, rows),
        pattern.T,
        norm_gain.reshape(1, width),
        qkv_weight,
        out_weight,
        grad_out,
    )
    out, grad_input, grad_qkv, grad_proj, grad_gain = pl.pallas_call(
        hand_out,
        out_shape=(out_shape, out_shape, qkv_shape, proj_shape, gain_shape),
        in_specs=[hbm] * 4,
        out_specs=(hbm,) * 5,
        scratch_shapes=[
            pltpu.VMEM((rows, width), BF16),
            pltpu.VMEM((rows, width), BF16),
            pltpu.VMEM((CORES, n // CORES, 4, width // n, LANES), BF16),
            pltpu.VMEM((1, width), F32),
            pltpu.VMEM((3, width, LANES), F32),
            pltpu.VMEM((LANES, width), F32),
            pltpu.SemaphoreType.DMA((13,)),
        ],
        compiler_params=pltpu.CompilerParams(vmem_limit_bytes=VMEM_LIMIT),
        name="hand_out",
    )(out.reshape(rows, width), grad_input.reshape(rows, width), grads, gain)
    return out, grad_input, grad_qkv, grad_proj, grad_gain.reshape(width)


def solution(mesh):
    return jax.shard_map(
        functools.partial(body, mesh.shape["pts"], mesh.shape["tp"]),
        mesh=mesh,
        in_specs=(
            P("pts", None),
            P("pts", None),
            P("pts", None),
            P(),
            P(None, None, "tp"),
            P("tp", None),
            P("pts", None),
        ),
        out_specs=(P("pts", None), P("pts", None), P(None, None, "tp"), P("tp", None), P()),
        check_vma=False,
    )
```
